256 devices in a mesh: grp: 16 (over z, y_lo), head: 16 (over x, y_hi, core).
Axes of the slice: x: 4, y: 4 (y_hi: 2, y_lo: 2; y = y_hi * 2 + y_lo), z: 8, core: 2. Of those that a mesh axis runs over, the one named last changes fastest.
Arguments:
- queries: bfloat16 [16, 192, 24576], P('grp', 'head'), may hold values from -8 to 8
- span_latent: bfloat16 [16, 192, 512], P('grp', 'head'), may hold values from -6 to 6
- span_rope: bfloat16 [16, 192, 64], P('grp', 'head'), may hold values from -6 to 6
- pool_latent: bfloat16 [8192, 8, 512], P(('grp', 'head')), may hold values from -6 to 6
- pool_rope: bfloat16 [8192, 512], P(('grp', 'head')), may hold values from -8 to 8
- page_table: int32 [16, 256], replicated, may hold values from 0 to 8191, as said below
- cache_len: int32 [16], replicated, may hold values from 512 to 2048, as said below
- span_len: int32 [16], replicated, may hold values from 48 to 192, as said below
- kv_up: bfloat16 [512, 32768], P(None, 'head'), may hold values from -0.375 to 0.375
- out_weight: bfloat16 [16384, 7168], P('head', 'grp'), may hold values from -0.046875 to 0.046875
Outputs:
- layer_out: bfloat16 [16, 192, 7168], P('grp', 'head')
The draws below stay inside these ranges and needn't reach their ends.
Inputs may be any that keep to these rules, and one draw needn't show every extreme that they name: `page_table`: entries are distinct pool slots; slot t lies on pool device t // 32, devices numbered along grp then head. No request has more than 2 pages on one pool device, and every request has exactly 2 on some device. `cache_len`: some request has exactly 2048. `span_len`: some request has exactly 192.
All inputs are finite; a program needn't handle non-finite values.
Results may differ from the reference program's by a relative error of at most 0.02.
Values may be sent and summed in bfloat16 or wider, within the bound.
No kernel may reach another device: no remote copies, remote signals or barrier semaphores. Data moves between devices by JAX's collectives and lax.ppermute only.
A program may use at most 128 MiB of HBM per device.

```python
import jax
import jax.numpy as jnp
from jax import lax

D = 7168
HEADS = 128
LATENT = 512
ROPE = 64
NOPE = 128
VDIM = 128
PAGE = 8
SPAN = 192
NPAGES = 256
CTX = 2048
SLOTS = 32
N_GRP = 16
N_HEAD = 16
DEVICES = 256


def draw_queries(key, part):
    key = jax.random.fold_in(key, 11)
    shape = (N_GRP, SPAN, HEADS, NOPE + ROPE)
    values = jnp.clip(jax.random.normal(key, shape, jnp.float32), -6.0, 6.0)
    return values.reshape(N_GRP, SPAN, HEADS * (NOPE + ROPE)).astype(jnp.bfloat16)


def draw_pool_rope(key, part):
    key = jax.random.fold_in(key, 13)
    shape = (DEVICES * SLOTS, PAGE, ROPE)
    values = jnp.clip(jax.random.normal(key, shape, jnp.float32), -6.0, 6.0)
    return values.reshape(DEVICES * SLOTS, PAGE * ROPE).astype(jnp.bfloat16)


def draw_page_table(key, part):
    key = jax.random.fold_in(key, 5)
    first_key, second_key = jax.random.split(key)
    requests = jnp.arange(N_GRP)
    devices_of = jax.vmap(lambda index: jax.random.permutation(jax.random.fold_in(first_key, index), DEVICES))(requests)
    pages = jnp.arange(NPAGES)
    owner = devices_of[:, pages // 2]
    slot_orders = jax.vmap(lambda index: jax.random.permutation(jax.random.fold_in(second_key, index), SLOTS))(jnp.arange(DEVICES))
    local_slot = slot_orders[owner, 2 * requests[:, None] + (pages % 2)[None, :]]
    return (owner * SLOTS + local_slot).astype(jnp.int32)


def draw_cache_len(key, part):
    key = jax.random.fold_in(key, 17)
    first_key, second_key = jax.random.split(key)
    lengths = jax.random.randint(first_key, (N_GRP,), CTX // 4, CTX + 1)
    longest = jax.random.randint(second_key, (), 0, N_GRP)
    return jnp.where(jnp.arange(N_GRP) == longest, CTX, lengths).astype(jnp.int32)


def draw_span_len(key, part):
    key = jax.random.fold_in(key, 19)
    first_key, second_key = jax.random.split(key)
    lengths = jax.random.randint(first_key, (N_GRP,), SPAN // 4, SPAN + 1)
    longest = jax.random.randint(second_key, (), 0, N_GRP)
    return jnp.where(jnp.arange(N_GRP) == longest, SPAN, lengths).astype(jnp.int32)


def block_levels(rng, dims, cuts, low, top_value):
    gain, own = 1.0, jax.random.fold_in(rng, 6)
    for position, shards_of in cuts:
        heights = jnp.exp(jax.random.uniform(jax.random.fold_in(own, position), (shards_of,), jnp.float32, low / len(cuts), top_value / len(cuts)))
        gain = gain * jnp.repeat(heights, dims[position] // shards_of).reshape([-1 if axis == position else 1 for axis in range(len(dims))])
    return gain


def normal_values(rng, extent, deviation, limit, cuts=(), kind=jnp.bfloat16):
    entries = deviation * jax.random.normal(rng, extent, jnp.float32)
    if cuts:
        entries = entries * block_levels(rng, extent, cuts, -0.22, 0.18)
    return jnp.clip(entries, -limit, limit).astype(kind)


def setup_inputs(seed: int = 0) -> dict:
    key_list = jax.random.split(jax.random.key(seed), 11)
    queries = draw_queries(jax.random.fold_in(key_list[10], 71), 0)
    span_latent = normal_values(key_list[1], (N_GRP, SPAN, LATENT), 1.0, 6.0, ((0, 16), (1, 16)))
    span_rope = normal_values(key_list[2], (N_GRP, SPAN, ROPE), 1.0, 6.0, ((0, 16), (1, 16)))
    pool_latent = normal_values(key_list[3], (DEVICES * SLOTS, PAGE, LATENT), 1.0, 6.0, ((0, 256),))
    pool_rope = draw_pool_rope(jax.random.fold_in(key_list[10], 71), 0)
    page_table = draw_page_table(jax.random.fold_in(key_list[10], 71), 0)
    cache_len = draw_cache_len(jax.random.fold_in(key_list[10], 71), 0)
    span_len = draw_span_len(jax.random.fold_in(key_list[10], 71), 0)
    kv_up = normal_values(key_list[8], (LATENT, HEADS * (NOPE + VDIM)), 256 ** -0.5, 0.375, ((1, 16),))
    out_weight = normal_values(key_list[9], (HEADS * VDIM, D), (HEADS * VDIM) ** -0.5, 0.046875, ((0, 16), (1, 16)))
    return {"queries": queries, "span_latent": span_latent, "span_rope": span_rope, "pool_latent": pool_latent, "pool_rope": pool_rope, "page_table": page_table, "cache_len": cache_len, "span_len": span_len, "kv_up": kv_up, "out_weight": out_weight}


def round_half(values):
    return lax.optimization_barrier(values.astype(jnp.bfloat16)).astype(jnp.float32)


def reference(queries, span_latent, span_rope, pool_latent, pool_rope, page_table, cache_len, span_len, kv_up, out_weight):
    width = NOPE + ROPE
    score_scale = width ** -0.5
    block_heads = HEADS // N_HEAD
    up_view = kv_up.astype(jnp.float32).reshape(LATENT, N_HEAD, block_heads, NOPE + VDIM)
    key_blocks = jnp.transpose(up_view[..., :NOPE], (1, 0, 2, 3))
    value_blocks = jnp.transpose(up_view[..., NOPE:], (1, 0, 2, 3))
    rows = jnp.arange(SPAN, dtype=jnp.int32)
    places = jnp.arange(CTX + SPAN, dtype=jnp.int32)

    def one_group(items):
        query, latent, rope, tables, cached, appended = items
        key_latent = jnp.concatenate([pool_latent[tables].reshape(CTX, LATENT), latent], 0).astype(jnp.float32)
        key_rope = jnp.concatenate([pool_rope[tables].reshape(CTX, ROPE), rope], 0).astype(jnp.float32)
        visible = jnp.where(places[None, :] < CTX, places[None, :] < cached, places[None, :] - CTX <= rows[:, None])
        heads_view = query.astype(jnp.float32).reshape(SPAN, N_HEAD, block_heads, width)
        heads_view = jnp.transpose(heads_view, (1, 0, 2, 3))

        def head_block(blocks):
            query_block, key_up, value_up = blocks
            absorbed = round_half(jnp.einsum("rhn,chn->rhc", query_block[..., :NOPE], key_up))
            scores = jnp.einsum("rhc,kc->rhk", absorbed, key_latent)
            scores = scores + jnp.einsum("rhe,ke->rhk", query_block[..., NOPE:], key_rope)
            scores = jnp.where(visible[:, None, :], scores * score_scale, -jnp.inf)
            highest = jnp.max(scores, axis=-1, keepdims=True)
            expo = jnp.exp(scores - highest)
            weights = round_half(expo / jnp.sum(expo, axis=-1, keepdims=True))
            mixed_latent = round_half(jnp.einsum("rhk,kc->rhc", weights, key_latent))
            return jnp.einsum("rhc,chv->rhv", mixed_latent, value_up)

        outputs = lax.map(head_block, (heads_view, key_blocks, value_blocks))
        attended = jnp.transpose(outputs, (1, 0, 2, 3)).reshape(SPAN, HEADS * VDIM)
        attended = jnp.where(rows[:, None] < appended, attended, 0.0).astype(jnp.bfloat16)
        return jnp.dot(attended, out_weight, preferred_element_type=jnp.float32).astype(jnp.bfloat16)

    return lax.map(one_group, (queries, span_latent, span_rope, page_table, cache_len, span_len))
```

```python
import functools

import jax
import jax.numpy as jnp
import numpy as np
from jax import lax
from jax.experimental import pallas as pl
from jax.experimental.pallas import tpu as pltpu
from jax.sharding import Mesh
from jax.sharding import PartitionSpec as P

LATENT = 512
ROPE = 64
NOPE = 128
VDIM = 128
PAGE = 8
CAP = 2
WIDTH = LATENT + ROPE
QHEAD = NOPE + ROPE
HEADS_HERE = 8
SPAN = 192
OWN = 12
CTX = 2048
KEYS = CTX + SPAN
BF = jnp.bfloat16
F32 = jnp.float32
NEG = -1e30
LOG2E = 1.4426950408889634


def step(axis, count, by):
    def send(value):
        return lax.ppermute(value, axis, [(i, (i + by) % count) for i in range(count)])

    return send


def split_body(q_ref, o_ref):
    for part in range(4):
        o_ref[part] = q_ref[:, part * 1536 : (part + 1) * 1536]


def split_queries(q):
    return pl.pallas_call(
        split_body,
        grid=(4,),
        in_specs=[pl.BlockSpec((OWN, 4 * 1536), lambda i: (0, i))],
        out_specs=pl.BlockSpec((4, OWN, 1536), lambda i: (i, 0, 0)),
        out_shape=jax.ShapeDtypeStruct((16, OWN, 1536), BF),
        name="split_queries",
    )(q)


CHUNKS = [(0, 512), (512, 512), (1024, 512), (1536, 512), (2048, 192)]


def attend_body(lens_ref, q_ref, up_ref, key_ref, o_ref, qcat, scores):
    cached = lens_ref[0]
    appended = lens_ref[1]
    scale = LOG2E * (QHEAD**-0.5)
    for h in range(2):
        rows = slice(h * SPAN, (h + 1) * SPAN)
        plain = q_ref[:, h * QHEAD : h * QHEAD + NOPE]
        key_up = up_ref[:, h * 256 : h * 256 + NOPE]
        qcat[rows, :LATENT] = lax.dot_general(
            plain, key_up, (((1,), (1,)), ((), ())), preferred_element_type=F32
        ).astype(BF)
        qcat[rows, LATENT:] = q_ref[:, h * QHEAD + NOPE : (h + 1) * QHEAD]
    query = qcat[...]
    highest = jnp.full((2 * SPAN, 1), NEG, F32)
    for start, size in CHUNKS:
        s = lax.dot_general(
            query, key_ref[start : start + size, :], (((1,), (1,)), ((), ())), preferred_element_type=F32
        )
        if start < CTX:
            at = start + lax.broadcasted_iota(jnp.int32, (1, size), 1)
            s = jnp.where(at < cached, s, NEG)
        else:
            row = lax.broadcasted_iota(jnp.int32, (SPAN, SPAN), 0)
            col = lax.broadcasted_iota(jnp.int32, (SPAN, SPAN), 1)
            bias = jnp.where(col <= row, 0.0, NEG).astype(F32)
            s = s + jnp.concatenate([bias, bias], 0)
        scores[:, start : start + size] = s
        highest = jnp.maximum(highest, jnp.max(s, axis=1, keepdims=True))
    total = jnp.zeros((2 * SPAN, 1), F32)
    mixed = jnp.zeros((2 * SPAN, LATENT), F32)
    shift = highest * scale
    for start, size in CHUNKS:
        p = jnp.exp2(scores[:, start : start + size] * scale - shift)
        total = total + jnp.sum(p, axis=1, keepdims=True)
        mixed = mixed + jnp.dot(
            p.astype(BF), key_ref[start : start + size, :LATENT], preferred_element_type=F32
        )
    mixed = (mixed / total).astype(BF)
    live = lax.broadcasted_iota(jnp.int32, (SPAN, 1), 0) < appended
    for h in range(2):
        value_up = up_ref[:, h * 256 + NOPE : (h + 1) * 256]
        out = jnp.dot(mixed[h * SPAN : (h + 1) * SPAN], value_up, preferred_element_type=F32)
        o_ref[:, h * VDIM : (h + 1) * VDIM] = jnp.where(live, out, 0.0).astype(BF)


def attend(lens, q, up, keys):
    return pl.pallas_call(
        attend_body,
        grid_spec=pltpu.PrefetchScalarGridSpec(
            num_scalar_prefetch=1,
            grid=(4,),
            in_specs=[
                pl.BlockSpec((SPAN, 2 * QHEAD), lambda i, s: (0, i)),
                pl.BlockSpec((LATENT, 512), lambda i, s: (0, i)),
                pl.BlockSpec((KEYS, WIDTH), lambda i, s: (0, 0)),
            ],
            out_specs=pl.BlockSpec((SPAN, 256), lambda i, s: (0, i)),
            scratch_shapes=[
                pltpu.VMEM((2 * SPAN, WIDTH), BF),
                pltpu.VMEM((2 * SPAN, KEYS), F32),
            ],
        ),
        out_shape=jax.ShapeDtypeStruct((SPAN, HEADS_HERE * VDIM), BF),
        compiler_params=pltpu.CompilerParams(vmem_limit_bytes=40 * 1024 * 1024),
        cost_estimate=pl.CostEstimate(
            flops=8_000_000_000, bytes_accessed=6_000_000, transcendentals=3_500_000
        ),
        name="attend",
    )(lens, q, up, keys)


def project_body(own_ref, mate_ref, w_ref, o_ref):
    nt = (((1,), (1,)), ((), ()))
    for half in range(2):
        w_own = w_ref[:, :224, half * 512 : (half + 1) * 512].reshape(896, 512)
        w_mate = w_ref[:, 224:, half * 512 : (half + 1) * 512].reshape(896, 512)
        part = lax.dot_general(
            own_ref[:, half * 512 : (half + 1) * 512], w_own, nt, preferred_element_type=F32
        ) + lax.dot_general(
            mate_ref[:, half * 512 : (half + 1) * 512], w_mate, nt, preferred_element_type=F32
        )
        total = part if half == 0 else total + part
    for request in range(2):
        for place in range(8):
            at = request * SPAN + place * 24
            o_ref[place, request] = total[at : at + 24].astype(BF)


def project(own, mate, weight):
    return pl.pallas_call(
        project_body,
        grid=(2,),
        in_specs=[
            pl.BlockSpec((2 * SPAN, 1024), lambda i: (0, 0)),
            pl.BlockSpec((2 * SPAN, 1024), lambda i: (0, 0)),
            pl.BlockSpec((4, 448, 1024), lambda i: (i, 0, 0)),
        ],
        out_specs=pl.BlockSpec((8, 2, 24, 896), lambda i: (0, 0, 0, i)),
        out_shape=jax.ShapeDtypeStruct((8, 2, 24, 1792), BF),
        compiler_params=pltpu.CompilerParams(vmem_limit_bytes=40 * 1024 * 1024),
        name="project",
    )(own, mate, weight)


def shards(
    queries,
    span_latent,
    span_rope,
    pool_latent,
    pool_rope,
    page_table,
    cache_len,
    span_len,
    kv_up,
    out_weight,
):
    zi, yl, xi, yh, ci = (lax.axis_index(a) for a in ("z", "yl", "x", "yh", "c"))
    group = zi * 2 + yl
    member = (xi * 2 + yh) * 2 + ci
    device = group * 16 + member
    slots = pool_latent.shape[0]
    pages = page_table.shape[1]
    swap_c = step("c", 2, 1)
    swap_yl = step("yl", 2, 1)
    swap_yh = step("yh", 2, 1)

    turned = out_weight.T
    kept = lax.dynamic_slice_in_dim(turned, ci * 224, 224, 0)
    given = lax.dynamic_slice_in_dim(turned, (1 - ci) * 224, 224, 0)
    columns = jnp.concatenate([kept, swap_c(given)], 0)
    weight = lax.all_gather(columns, "z", axis=0, tiled=False)

    owners = page_table // slots
    slot_of = page_table % slots
    owned = (owners == device).astype(jnp.int32)
    ranking = jnp.cumsum(owned, axis=1) - 1
    chosen = (owned[:, None, :] == 1) & (
        ranking[:, None, :] == jnp.arange(CAP, dtype=jnp.int32)[None, :, None]
    )
    send_slot = jnp.sum(jnp.where(chosen, slot_of[:, None, :], 0), axis=2)
    filled = jnp.any(chosen, axis=2)
    pool = jnp.concatenate([pool_latent, pool_rope.reshape(slots, PAGE, ROPE)], 2)
    send = jnp.where(filled[:, :, None, None], pool[send_slot], jnp.zeros((), BF))
    send = send.reshape(16, 1, CAP * PAGE, WIDTH)
    send = jnp.broadcast_to(send, (16, 2, CAP * PAGE, WIDTH)).reshape(32, CAP * PAGE, WIDTH)
    back = lax.all_to_all(send, ("z", "yl", "yh"), split_axis=0, concat_axis=0, tiled=True)

    fresh = jnp.concatenate([span_latent[0], span_rope[0]], 1)
    fresh = jnp.pad(fresh, ((0, 4), (0, 0)))
    mine = jnp.concatenate([back.reshape(512, WIDTH), fresh, swap_yh(fresh)], 0)
    half = mine.shape[0] // 2
    left = step("x", 4, 1)(mine)
    right = step("x", 4, -1)(mine)
    far_a = step("x", 4, 1)(left[:half])
    far_b = step("x", 4, -1)(right[half:])

    sent = split_queries(queries[0])
    exchanged = lax.all_to_all(sent, ("x", "yh", "c"), split_axis=0, concat_axis=0, tiled=True)
    q = exchanged.reshape(SPAN, HEADS_HERE * QHEAD)

    column = jnp.concatenate([mine, left, right, far_a, far_b], 0)
    both = jnp.concatenate([column, swap_c(column)], 0).reshape(8, 68, PAGE, WIDTH)
    piece_of = jnp.array([0, 2, 3, 1], jnp.int32)
    my_table = lax.dynamic_index_in_dim(page_table, group, 0, keepdims=False)
    source = my_table // slots
    order = jnp.arange(pages, dtype=jnp.int32)
    before = (source[None, :] == source[:, None]) & (order[None, :] < order[:, None])
    place = jnp.sum(before.astype(jnp.int32), axis=1)
    from_group = source // 16
    from_member = source % 16
    from_x = from_member // 4
    from_yh = (from_member // 2) % 2
    from_c = from_member % 2
    block = jnp.where(from_c == ci, 0, 4) + piece_of[(from_x - xi) % 4]
    flat = block * 68 + (from_group * 2 + from_yh) * CAP + place
    cache = both.reshape(8 * 68, PAGE, WIDTH)[flat].reshape(CTX, WIDTH)
    heads16 = jnp.arange(16, dtype=jnp.int32)
    block16 = jnp.where(heads16 % 2 == ci, 0, 4) + piece_of[(heads16 // 4 - xi) % 4]
    which = jnp.where((heads16 // 2) % 2 == yh, 0, 1)
    news = both[:, 64:].reshape(16, 16, WIDTH)[block16 * 2 + which][:, :OWN].reshape(SPAN, WIDTH)
    keys = jnp.concatenate([cache, news], 0)

    lens = jnp.stack(
        [
            lax.dynamic_index_in_dim(cache_len, group, 0, keepdims=False),
            lax.dynamic_index_in_dim(span_len, group, 0, keepdims=False),
        ]
    )
    attended = attend(lens, q, kv_up, keys)
    own = jnp.concatenate([attended, swap_yl(attended)], 0)
    mate = swap_c(own)
    partial = project(own, mate, weight)
    shared = lax.all_to_all(partial, ("x", "yh"), split_axis=0, concat_axis=0, tiled=True)
    summed = jnp.sum(shared.astype(F32), axis=0).astype(BF)
    summed = summed.reshape(2, 2, OWN, 1792)
    own_rows = lax.dynamic_index_in_dim(summed, ci, 1, keepdims=False)
    mate_rows = lax.dynamic_index_in_dim(summed, 1 - ci, 1, keepdims=False)
    here = own_rows[0]
    from_c = swap_c(mate_rows[0])
    from_yl = swap_yl(own_rows[1])
    from_both = lax.ppermute(mate_rows[1], ("yl", "c"), [(i, 3 - i) for i in range(4)])
    same = jnp.stack([here, from_c])
    other = jnp.stack([from_yl, from_both])
    first = jnp.where(yl == 0, same, other)
    second = jnp.where(yl == 0, other, same)
    grid = jnp.stack([first, second])
    grid = jnp.where(ci == 0, grid, grid[:, ::-1])
    grid = grid.reshape(2, 2, OWN, 8, 224)
    out = jnp.transpose(grid, (2, 3, 0, 1, 4)).reshape(OWN, 7168)
    return out[None]


def solution(mesh):
    fine = Mesh(mesh.devices.reshape(8, 2, 4, 2, 2), ("z", "yl", "x", "yh", "c"))
    grp, head = ("z", "yl"), ("x", "yh", "c")
    return jax.shard_map(
        shards,
        mesh=fine,
        in_specs=(
            P(grp, head, None),
            P(grp, head, None),
            P(grp, head, None),
            P(grp + head, None, None),
            P(grp + head, None),
            P(),
            P(),
            P(),
            P(None, head),
            P(head, grp),
        ),
        out_specs=P(grp, head, None),
        check_vma=False,
    )
```

```python
import jax
import jax.numpy as jnp
from jax import lax
from jax.experimental import pallas as pl
from jax.experimental.pallas import tpu as pltpu
from jax.sharding import Mesh
from jax.sharding import PartitionSpec as P

LATENT = 512
ROPE = 64
NOPE = 128
VDIM = 128
PAGE = 8
QHEAD = NOPE + ROPE
HEADS_HERE = 8
SPAN = 192
OWN = 12
CTX = 2048
BF = jnp.bfloat16
F32 = jnp.float32
NEG = -1e30
LOG2E = 1.4426950408889634


def step(axis, count, by):
    def send(value):
        return lax.ppermute(value, axis, [(i, (i + by) % count) for i in range(count)])

    return send


def split_body(q_ref, o_ref):
    for part in range(4):
        o_ref[part] = q_ref[:, part * 1536 : (part + 1) * 1536]


def split_queries(q):
    return pl.pallas_call(
        split_body,
        grid=(4,),
        in_specs=[pl.BlockSpec((OWN, 4 * 1536), lambda i: (0, i))],
        out_specs=pl.BlockSpec((4, OWN, 1536), lambda i: (i, 0, 0)),
        out_shape=jax.ShapeDtypeStruct((16, OWN, 1536), BF),
        name="split_queries",
    )(q)


PIECE = 34
CHUNKS = [(0, 512), (512, 512), (1024, 512), (1536, 512), (2048, 256)]
ALLKEYS = CTX + 256
KWIDTH = LATENT + 2 * ROPE


def tiles_of(page):
    return jnp.concatenate([page[:, j * 128 : (j + 1) * 128] for j in range(4)], 0)


def pack_body(slot_ref, pool_ref, rope_ref, span_ref, span_rope_ref, o_ref, f_ref):
    def one(dest, carry):
        first = slot_ref[2 * dest]
        second = slot_ref[2 * dest + 1]
        tiles = jnp.concatenate([tiles_of(pool_ref[first]), tiles_of(pool_ref[second])], 0)
        rope = jnp.concatenate([rope_ref[first], rope_ref[second]], 1)
        for copy in range(2):
            o_ref[2 * dest + copy, :64] = tiles
            o_ref[2 * dest + copy, 64:] = rope
        return carry

    lax.fori_loop(0, 16, one, 0)
    for k in range(2):
        f_ref[k, :64] = jnp.concatenate([tiles_of(span_ref[k, :8]), tiles_of(span_ref[k, 8:])], 0)
        f_ref[k, 64:] = jnp.concatenate([span_rope_ref[k, :8], span_rope_ref[k, 8:]], 1)


def pack(slots, pool, rope, span, span_rope):
    vmem = pl.BlockSpec(memory_space=pltpu.VMEM)
    return pl.pallas_call(
        pack_body,
        in_specs=[pl.BlockSpec(memory_space=pltpu.SMEM), vmem, vmem, vmem, vmem],
        out_specs=[vmem, vmem],
        out_shape=[
            jax.ShapeDtypeStruct((32, 72, 128), BF),
            jax.ShapeDtypeStruct((2, 72, 128), BF),
        ],
        name="pack",
    )(slots, pool, rope, span, span_rope)


PLACES = ((0, 34), (34, 34), (68, 34), (102, 17), (119, 17))


def attend_body(lens_ref, index_ref, q_ref, up_ref, *rest):
    pieces = rest[:10]
    o_ref, held, keys, qcat, scores, sems = rest[10:]
    cached = lens_ref[0]
    appended = lens_ref[1]
    scale = LOG2E * (QHEAD**-0.5)

    @pl.when(pl.program_id(0) == 0)
    def assemble():
        copies = []
        for n, piece in enumerate(pieces):
            start, size = PLACES[n % 5]
            start += 136 * (n // 5)
            copies.append(pltpu.make_async_copy(piece, held.at[start : start + size], sems.at[n]))
        for copy in copies:
            copy.start()
        for copy in copies:
            copy.wait()
        lane_half = lax.broadcasted_iota(jnp.int32, (8, 128), 1) // 64

        def pair(i, carry):
            lat, rope = [], []
            for k in range(2):
                at = index_ref[2 * i + k]
                block = at // 2
                place = at % 2
                lat.append(held[block, pl.ds(pl.multiple_of(place * 32, 32), 32), :])
                rope.append(jnp.where(lane_half == place, held[block, 64:72, :], jnp.zeros((), BF)))
            rows = pl.ds(pl.multiple_of(i * 16, 16), 16)
            for j in range(4):
                keys[rows, j * 128 : (j + 1) * 128] = jnp.concatenate(
                    [lat[0][8 * j : 8 * j + 8], lat[1][8 * j : 8 * j + 8]], 0
                )
            keys[rows, LATENT:] = jnp.concatenate(rope, 0)
            return carry

        lax.fori_loop(0, ALLKEYS // 16, pair, 0, unroll=2)

    for h in range(2):
        rows = slice(h * SPAN, (h + 1) * SPAN)
        plain = q_ref[:, h * QHEAD : h * QHEAD + NOPE]
        key_up = up_ref[:, h * 256 : h * 256 + NOPE]
        qcat[rows, :LATENT] = lax.dot_general(
            plain, key_up, (((1,), (1,)), ((), ())), preferred_element_type=F32
        ).astype(BF)
        rope = q_ref[:, h * QHEAD + NOPE : (h + 1) * QHEAD]
        qcat[rows, LATENT:] = jnp.concatenate([rope, rope], 1)
    query = qcat[...]
    highest = jnp.full((2 * SPAN, 1), NEG, F32)
    for start, size in CHUNKS:
        s = lax.dot_general(
            query, keys[start : start + size, :], (((1,), (1,)), ((), ())), preferred_element_type=F32
        )
        if start < CTX:
            at = start + lax.broadcasted_iota(jnp.int32, (1, size), 1)
            s = jnp.where(at < cached, s, NEG)
        else:
            row = lax.broadcasted_iota(jnp.int32, (SPAN, 256), 0)
            col = lax.broadcasted_iota(jnp.int32, (SPAN, 256), 1)
            token = col % 16
            seen = (token < OWN) & (col // 16 * OWN + token <= row)
            bias = jnp.where(seen, 0.0, NEG).astype(F32)
            s = s + jnp.concatenate([bias, bias], 0)
        scores[:, start : start + size] = s
        highest = jnp.maximum(highest, jnp.max(s, axis=1, keepdims=True))
    total = jnp.zeros((2 * SPAN, 1), F32)
    mixed = jnp.zeros((2 * SPAN, LATENT), F32)
    shift = highest * scale
    for start, size in CHUNKS:
        p = jnp.exp2(scores[:, start : start + size] * scale - shift)
        total = total + jnp.sum(p, axis=1, keepdims=True)
        mixed = mixed + jnp.dot(
            p.astype(BF), keys[start : start + size, :LATENT], preferred_element_type=F32
        )
    mixed = (mixed / total).astype(BF)
    live = lax.broadcasted_iota(jnp.int32, (SPAN, 1), 0) < appended
    for h in range(2):
        value_up = up_ref[:, h * 256 + NOPE : (h + 1) * 256]
        out = jnp.dot(mixed[h * SPAN : (h + 1) * SPAN], value_up, preferred_element_type=F32)
        o_ref[:, h * VDIM : (h + 1) * VDIM] = jnp.where(live, out, 0.0).astype(BF)


def attend(lens, index, q, up, pieces):
    return pl.pallas_call(
        attend_body,
        grid_spec=pltpu.PrefetchScalarGridSpec(
            num_scalar_prefetch=2,
            grid=(4,),
            in_specs=[
                pl.BlockSpec((SPAN, 2 * QHEAD), lambda i, *s: (0, i)),
                pl.BlockSpec((LATENT, 512), lambda i, *s: (0, i)),
            ]
            + [pl.BlockSpec(memory_space=pl.ANY)] * 10,
            out_specs=pl.BlockSpec((SPAN, 256), lambda i, *s: (0, i)),
            scratch_shapes=[
                pltpu.VMEM((8 * PIECE, 72, 128), BF),
                pltpu.VMEM((ALLKEYS, KWIDTH), BF),
                pltpu.VMEM((2 * SPAN, KWIDTH), BF),
                pltpu.VMEM((2 * SPAN, ALLKEYS), F32),
                pltpu.SemaphoreType.DMA((10,)),
            ],
        ),
        out_shape=jax.ShapeDtypeStruct((SPAN, HEADS_HERE * VDIM), BF),
        compiler_params=pltpu.CompilerParams(vmem_limit_bytes=40 * 1024 * 1024),
        cost_estimate=pl.CostEstimate(
            flops=8_000_000_000, bytes_accessed=6_000_000, transcendentals=3_500_000
        ),
        name="attend",
    )(lens, index, q, up, *pieces)


def project_body(own_ref, own_y_ref, mate_ref, mate_y_ref, w_ref, o_ref):
    nt = (((1,), (1,)), ((), ()))
    for request, (own, mate) in enumerate(((own_ref, mate_ref), (own_y_ref, mate_y_ref))):
        total = lax.dot_general(
            own[...], w_ref[:, :224].reshape(896, 1024), nt, preferred_element_type=F32
        ) + lax.dot_general(
            mate[...], w_ref[:, 224:].reshape(896, 1024), nt, preferred_element_type=F32
        )
        for place in range(8):
            o_ref[place, request] = total[place * 24 : (place + 1) * 24].astype(BF)


def project(own, own_y, mate, mate_y, weight):
    return pl.pallas_call(
        project_body,
        grid=(2,),
        in_specs=[pl.BlockSpec((SPAN, 1024), lambda i: (0, 0))] * 4
        + [pl.BlockSpec((4, 448, 1024), lambda i: (i, 0, 0))],
        out_specs=pl.BlockSpec((8, 2, 24, 896), lambda i: (0, 0, 0, i)),
        out_shape=jax.ShapeDtypeStruct((8, 2, 24, 1792), BF),
        compiler_params=pltpu.CompilerParams(vmem_limit_bytes=40 * 1024 * 1024),
        name="project",
    )(own, own_y, mate, mate_y, weight)


def total_body(where_ref, x_ref, *outs):
    core = where_ref[1]
    for request in range(2):
        value = jnp.sum(x_ref[:, request].astype(F32), axis=0)
        low, high = value[:OWN], value[OWN:]
        outs[2 * request][...] = jnp.where(core == 0, low, high).astype(BF)
        outs[2 * request + 1][...] = jnp.where(core == 0, high, low).astype(BF)


def total_parts(where, shared):
    vmem = pl.BlockSpec(memory_space=pltpu.VMEM)
    return pl.pallas_call(
        total_body,
        in_specs=[pl.BlockSpec(memory_space=pltpu.SMEM), vmem],
        out_specs=[vmem] * 4,
        out_shape=[jax.ShapeDtypeStruct((OWN, 1792), BF)] * 4,
        name="total_parts",
    )(where, shared)


def arrange_body(where_ref, here_ref, c_ref, y_ref, both_ref, o_ref):
    yl, core = where_ref[0], where_ref[1]
    here, mate, near, far = (r[...].astype(F32) for r in (here_ref, c_ref, y_ref, both_ref))
    same = (jnp.where(core == 0, here, mate), jnp.where(core == 0, mate, here))
    other = (jnp.where(core == 0, near, far), jnp.where(core == 0, far, near))
    parts = [jnp.where(yl == 0, same[k], other[k]) for k in range(2)]
    parts += [jnp.where(yl == 0, other[k], same[k]) for k in range(2)]
    for z in range(8):
        o_ref[:, z * 896 : (z + 1) * 896] = jnp.concatenate(
            [p[:, z * 224 : (z + 1) * 224] for p in parts], 1
        ).astype(BF)


def arrange(where, here, mate, near, far):
    vmem = pl.BlockSpec(memory_space=pltpu.VMEM)
    return pl.pallas_call(
        arrange_body,
        in_specs=[pl.BlockSpec(memory_space=pltpu.SMEM)] + [vmem] * 4,
        out_specs=vmem,
        out_shape=jax.ShapeDtypeStruct((OWN, 7168), BF),
        name="arrange",
    )(where, here, mate, near, far)


def shards(
    queries,
    span_latent,
    span_rope,
    pool_latent,
    pool_rope,
    page_table,
    cache_len,
    span_len,
    kv_up,
    out_weight,
):
    zi, yl, xi, yh, ci = (lax.axis_index(a) for a in ("z", "yl", "x", "yh", "c"))
    group = zi * 2 + yl
    member = (xi * 2 + yh) * 2 + ci
    device = group * 16 + member
    slots = pool_latent.shape[0]
    pages = page_table.shape[1]
    swap_c = step("c", 2, 1)
    swap_yl = step("yl", 2, 1)
    swap_yh = step("yh", 2, 1)

    owners = page_table // slots
    slot_of = page_table % slots
    order = jnp.arange(pages, dtype=jnp.int32)
    marked = order[None, :] * slots + slot_of
    owned = owners == device
    first = jnp.min(jnp.where(owned, marked, pages * slots), axis=1)
    last = jnp.max(jnp.where(owned, marked, 0), axis=1)
    picked = jnp.stack([first % slots, last % slots], 1).reshape(32)
    sent_pages, fresh = pack(
        picked,
        pool_latent,
        pool_rope.reshape(slots, PAGE, ROPE),
        jnp.pad(jnp.concatenate([span_latent, swap_yh(span_latent)], 0), ((0, 0), (0, 4), (0, 0))),
        jnp.pad(jnp.concatenate([span_rope, swap_yh(span_rope)], 0), ((0, 0), (0, 4), (0, 0))),
    )
    back = lax.all_to_all(sent_pages, ("z", "yl", "yh"), split_axis=0, concat_axis=0, tiled=True)

    turned = out_weight.T
    kept = lax.dynamic_slice_in_dim(turned, ci * 224, 224, 0)
    given = lax.dynamic_slice_in_dim(turned, (1 - ci) * 224, 224, 0)
    columns = jnp.concatenate([kept, swap_c(given)], 0)
    columns, back = lax.optimization_barrier((columns, back))
    weight = lax.all_gather(columns, "z", axis=0, tiled=False)

    mine = jnp.concatenate([back, fresh], 0)
    half = PIECE // 2
    left = step("x", 4, 1)(mine)
    right = step("x", 4, -1)(mine)

    sent = split_queries(queries[0])
    sent, back = lax.optimization_barrier((sent, back))
    exchanged = lax.all_to_all(sent, ("x", "yh", "c"), split_axis=0, concat_axis=0, tiled=True)
    q = exchanged.reshape(SPAN, HEADS_HERE * QHEAD)
    mine_c = swap_c(mine)
    left, right, q = lax.optimization_barrier((left, right, q))
    far_a = step("x", 4, 1)(left[:half])
    far_b = step("x", 4, -1)(right[half:])
    left_c, right_c = swap_c(left), swap_c(right)
    pieces = [mine, left, right, far_a, far_b, mine_c, left_c, right_c, swap_c(far_a), swap_c(far_b)]

    my_table = lax.dynamic_index_in_dim(page_table, group, 0, keepdims=False)
    source = my_table // slots
    before = (source[None, :] == source[:, None]) & (order[None, :] < order[:, None])
    place = jnp.minimum(jnp.sum(before.astype(jnp.int32), axis=1), 1)
    from_group = source // 16
    from_member = source % 16

    def piece_index(of_member):
        apart = (of_member // 4 - xi) % 4
        number = jnp.where(apart == 0, 0, jnp.where(apart == 3, 1, jnp.where(apart == 1, 2, 3)))
        return (jnp.where(of_member % 2 == ci, 0, 4) + number) * PIECE

    block = piece_index(from_member) + from_group * 2 + (from_member // 2) % 2
    members = jnp.arange(32, dtype=jnp.int32) // 2
    block_new = piece_index(members) + 32 + jnp.where((members // 2) % 2 == yh, 0, 1)
    index = jnp.concatenate([block * 2 + place, block_new * 2 + jnp.arange(32, dtype=jnp.int32) % 2])

    lens = jnp.stack(
        [
            lax.dynamic_index_in_dim(cache_len, group, 0, keepdims=False),
            lax.dynamic_index_in_dim(span_len, group, 0, keepdims=False),
        ]
    )
    attended = attend(lens, index, q, kv_up, pieces)
    near = swap_yl(attended)
    partial = project(attended, near, swap_c(attended), swap_c(near), weight)
    shared = lax.all_to_all(partial, ("x", "yh"), split_axis=0, concat_axis=0, tiled=True)
    where = jnp.stack([yl, ci]).astype(jnp.int32)
    here, to_c, to_yl, to_both = total_parts(where, shared)
    from_both = lax.ppermute(to_both, ("yl", "c"), [(i, 3 - i) for i in range(4)])
    out = arrange(where, here, swap_c(to_c), swap_yl(to_yl), from_both)
    return out[None]


def solution(mesh):
    fine = Mesh(mesh.devices.reshape(8, 2, 4, 2, 2), ("z", "yl", "x", "yh", "c"))
    grp, head = ("z", "yl"), ("x", "yh", "c")
    return jax.shard_map(
        shards,
        mesh=fine,
        in_specs=(
            P(grp, head, None),
            P(grp, head, None),
            P(grp, head, None),
            P(grp + head, None, None),
            P(grp + head, None),
            P(),
            P(),
            P(),
            P(None, head),
            P(head, grp),
        ),
        out_specs=P(grp, head, None),
        check_vma=False,
    )
```

```python
import jax
import jax.numpy as jnp
from jax import lax
from jax.experimental import pallas as pl
from jax.experimental.pallas import tpu as pltpu
from jax.sharding import Mesh
from jax.sharding import PartitionSpec as P

LATENT = 512
ROPE = 64
NOPE = 128
VDIM = 128
PAGE = 8
QHEAD = NOPE + ROPE
HEADS_HERE = 8
SPAN = 192
OWN = 12
CTX = 2048
BF = jnp.bfloat16
F32 = jnp.float32
NEG = -1e30
LOG2E = 1.4426950408889634


def step(axis, count, by):
    def send(value):
        return lax.ppermute(value, axis, [(i, (i + by) % count) for i in range(count)])

    return send


def split_body(q_ref, o_ref):
    for part in range(16):
        o_ref[part] = q_ref[:, part * 1536 : (part + 1) * 1536]


def split_queries(q):
    vmem = pl.BlockSpec(memory_space=pltpu.VMEM)
    return pl.pallas_call(
        split_body,
        in_specs=[vmem],
        out_specs=vmem,
        out_shape=jax.ShapeDtypeStruct((16, OWN, 1536), BF),
        name="split_queries",
    )(q)


PIECE = 34
NT = (((1,), (1,)), ((), ()))
VMEM_BYTES = 56 * 1024 * 1024
ALLKEYS = CTX + 256
KWIDTH = LATENT + 2 * ROPE


def tiles_of(page):
    return jnp.concatenate([page[:, j * 128 : (j + 1) * 128] for j in range(4)], 0)


def pack_body(slot_ref, pool_ref, rope_ref, o_ref):
    def one(dest, carry):
        first = slot_ref[2 * dest]
        second = slot_ref[2 * dest + 1]
        tiles = jnp.concatenate([tiles_of(pool_ref[first]), tiles_of(pool_ref[second])], 0)
        rope = jnp.concatenate([rope_ref[first], rope_ref[second]], 1)
        for copy in range(2):
            o_ref[2 * dest + copy, :64] = tiles
            o_ref[2 * dest + copy, 64:] = rope
        return carry

    lax.fori_loop(0, 16, one, 0, unroll=2)


def pack(slots, pool, rope):
    vmem = pl.BlockSpec(memory_space=pltpu.VMEM)
    return pl.pallas_call(
        pack_body,
        in_specs=[pl.BlockSpec(memory_space=pltpu.SMEM), vmem, vmem],
        out_specs=vmem,
        out_shape=jax.ShapeDtypeStruct((32, 72, 128), BF),
        name="pack",
    )(slots, pool, rope)


def fresh_body(span_ref, span_rope_ref, pair_ref, pair_rope_ref, f_ref):
    gap = jnp.zeros((4, LATENT), F32)
    gap_rope = jnp.zeros((4, ROPE), F32)
    for k, (lat, rope) in enumerate(((span_ref, span_rope_ref), (pair_ref, pair_rope_ref))):
        x = jnp.concatenate([lat[0].astype(F32), gap], 0)
        y = jnp.concatenate([rope[0].astype(F32), gap_rope], 0)
        f_ref[k, :64] = jnp.concatenate([tiles_of(x[:8]), tiles_of(x[8:])], 0).astype(BF)
        f_ref[k, 64:] = jnp.concatenate([y[:8], y[8:]], 1).astype(BF)


def pack_fresh(*spans):
    vmem = pl.BlockSpec(memory_space=pltpu.VMEM)
    return pl.pallas_call(
        fresh_body,
        in_specs=[vmem] * 4,
        out_specs=vmem,
        out_shape=jax.ShapeDtypeStruct((2, 72, 128), BF),
        name="pack_fresh",
    )(*spans)


PLACES = ((0, 34), (34, 34), (68, 34), (102, 17), (119, 17))


def assemble_body(index_ref, *rest):
    pieces, keys, held, sems = rest[:10], rest[10], rest[11], rest[12]
    copies = []
    for n, piece in enumerate(pieces):
        start, size = PLACES[n % 5]
        start += 136 * (n // 5)
        copies.append(pltpu.make_async_copy(piece, held.at[start : start + size], sems.at[n]))
    for copy in copies:
        copy.start()
    for copy in copies:
        copy.wait()
    lane_half = lax.broadcasted_iota(jnp.int32, (8, 128), 1) // 64

    def pair(i, carry):
        lat, rope = [], []
        for k in range(2):
            at = index_ref[2 * i + k]
            block = at // 2
            place = at % 2
            lat.append(held[block, pl.ds(pl.multiple_of(place * 32, 32), 32), :])
            rope.append(jnp.where(lane_half == place, held[block, 64:72, :], jnp.zeros((), BF)))
        rows = pl.ds(pl.multiple_of(i * 16, 16), 16)
        for j in range(4):
            keys[rows, j * 128 : (j + 1) * 128] = jnp.concatenate(
                [lat[0][8 * j : 8 * j + 8], lat[1][8 * j : 8 * j + 8]], 0
            )
        keys[rows, LATENT:] = jnp.concatenate(rope, 0)
        return carry

    lax.fori_loop(0, ALLKEYS // 16, pair, 0, unroll=4)


def assemble(index, pieces):
    return pl.pallas_call(
        assemble_body,
        in_specs=[pl.BlockSpec(memory_space=pltpu.SMEM)] + [pl.BlockSpec(memory_space=pl.ANY)] * 10,
        out_specs=pl.BlockSpec(memory_space=pltpu.VMEM),
        out_shape=jax.ShapeDtypeStruct((ALLKEYS, KWIDTH), BF),
        scratch_shapes=[
            pltpu.VMEM((8 * PIECE, 72, 128), BF),
            pltpu.SemaphoreType.DMA((10,)),
        ],
        compiler_params=pltpu.CompilerParams(vmem_limit_bytes=24 * 1024 * 1024),
        cost_estimate=pl.CostEstimate(flops=0, bytes_accessed=16_000_000, transcendentals=0),
        name="assemble",
    )(index, *pieces)


def attend_body(lens_ref, q_ref, up_ref, keys, o_ref, qcat, causal):
    cached = lens_ref[0]
    appended = lens_ref[1]
    scale = LOG2E * (QHEAD**-0.5)

    @pl.when(pl.program_id(0) == 0)
    def prepare():
        row = lax.broadcasted_iota(jnp.int32, (SPAN, 256), 0)
        col = lax.broadcasted_iota(jnp.int32, (SPAN, 256), 1)
        token = col % 16
        seen = (token < OWN) & (col // 16 * OWN + token <= row)
        causal[...] = jnp.where(seen, 0.0, NEG).astype(F32)

    for h in range(2):
        rows = slice(h * SPAN, (h + 1) * SPAN)
        plain = q_ref[:, h * QHEAD : h * QHEAD + NOPE]
        key_up = up_ref[:, h * 256 : h * 256 + NOPE]
        qcat[rows, :LATENT] = lax.dot_general(plain, key_up, NT, preferred_element_type=F32).astype(BF)
        rope = q_ref[:, h * QHEAD + NOPE : (h + 1) * QHEAD]
        qcat[rows, LATENT:] = jnp.concatenate([rope, rope], 1)
    s = lax.dot_general(qcat[...], keys[...], NT, preferred_element_type=F32)
    at = lax.broadcasted_iota(jnp.int32, (1, CTX), 1)
    s = jnp.concatenate(
        [
            s[:, :CTX] + jnp.where(at < cached, 0.0, NEG),
            s[:, CTX:] + jnp.concatenate([causal[...], causal[...]], 0),
        ],
        1,
    )
    highest = jnp.max(s, axis=1, keepdims=True)
    p = jnp.exp2((s - highest) * scale)
    total = jnp.sum(p, axis=1, keepdims=True)
    mixed = jnp.dot(p.astype(BF), keys[:, :LATENT], preferred_element_type=F32)
    mixed = (mixed / total).astype(BF)
    live = lax.broadcasted_iota(jnp.int32, (SPAN, 1), 0) < appended
    for h in range(2):
        value_up = up_ref[:, h * 256 + NOPE : (h + 1) * 256]
        out = jnp.dot(mixed[h * SPAN : (h + 1) * SPAN], value_up, preferred_element_type=F32)
        o_ref[:, h * VDIM : (h + 1) * VDIM] = jnp.where(live, out, 0.0).astype(BF)


def attend(half, lens, q, up, keys):
    return pl.pallas_call(
        attend_body,
        grid_spec=pltpu.PrefetchScalarGridSpec(
            num_scalar_prefetch=1,
            grid=(2,),
            in_specs=[
                pl.BlockSpec((SPAN, 2 * QHEAD), lambda i, s: (0, 2 * half + i)),
                pl.BlockSpec((LATENT, 512), lambda i, s: (0, 2 * half + i)),
                pl.BlockSpec((ALLKEYS, KWIDTH), lambda i, s: (0, 0)),
            ],
            out_specs=pl.BlockSpec((SPAN, 256), lambda i, s: (0, i)),
            scratch_shapes=[
                pltpu.VMEM((2 * SPAN, KWIDTH), BF),
                pltpu.VMEM((SPAN, 256), F32),
            ],
        ),
        out_shape=jax.ShapeDtypeStruct((SPAN, 512), BF),
        compiler_params=pltpu.CompilerParams(vmem_limit_bytes=40 * 1024 * 1024),
        cost_estimate=pl.CostEstimate(
            flops=5_000_000_000, bytes_accessed=4_000_000, transcendentals=1_800_000
        ),
        name="attend",
    )(lens, q, up, keys)


def project_body(*refs):
    parts, w_ref, o_ref = refs[:8], refs[8], refs[9]
    own, near, mate, mate_near = (
        jnp.concatenate([parts[2 * k][...], parts[2 * k + 1][...]], 1) for k in range(4)
    )
    total = lax.dot_general(
        jnp.concatenate([own, near], 0),
        w_ref[:, :224].reshape(896, 1024),
        NT,
        preferred_element_type=F32,
    ) + lax.dot_general(
        jnp.concatenate([mate, mate_near], 0),
        w_ref[:, 224:].reshape(896, 1024),
        NT,
        preferred_element_type=F32,
    )
    for request in range(2):
        for place in range(8):
            at = request * SPAN + place * 24
            o_ref[place, request] = total[at : at + 24].astype(BF)


def project(parts, weight):
    return pl.pallas_call(
        project_body,
        grid=(2,),
        in_specs=[pl.BlockSpec((SPAN, 512), lambda i: (0, 0))] * 8
        + [pl.BlockSpec((4, 448, 1024), lambda i: (i, 0, 0))],
        out_specs=pl.BlockSpec((8, 2, 24, 896), lambda i: (0, 0, 0, i)),
        out_shape=jax.ShapeDtypeStruct((8, 2, 24, 1792), BF),
        compiler_params=pltpu.CompilerParams(vmem_limit_bytes=VMEM_BYTES),
        name="project",
    )(*parts, weight)


def total_body(where_ref, x_ref, *outs):
    core = where_ref[1]
    for request in range(2):
        value = jnp.sum(x_ref[:, request].astype(F32), axis=0)
        low, high = value[:OWN], value[OWN:]
        outs[2 * request][...] = jnp.where(core == 0, low, high).astype(BF)
        outs[2 * request + 1][...] = jnp.where(core == 0, high, low).astype(BF)


def total_parts(where, shared):
    vmem = pl.BlockSpec(memory_space=pltpu.VMEM)
    return pl.pallas_call(
        total_body,
        in_specs=[pl.BlockSpec(memory_space=pltpu.SMEM), vmem],
        out_specs=[vmem] * 4,
        out_shape=[jax.ShapeDtypeStruct((OWN, 1792), BF)] * 4,
        name="total_parts",
    )(where, shared)


def arrange_body(where_ref, here_ref, c_ref, y_ref, both_ref, o_ref):
    yl, core = where_ref[0], where_ref[1]
    here, mate, near, far = (r[...].astype(F32) for r in (here_ref, c_ref, y_ref, both_ref))
    same = (jnp.where(core == 0, here, mate), jnp.where(core == 0, mate, here))
    other = (jnp.where(core == 0, near, far), jnp.where(core == 0, far, near))
    parts = [jnp.where(yl == 0, same[k], other[k]) for k in range(2)]
    parts += [jnp.where(yl == 0, other[k], same[k]) for k in range(2)]
    for z in range(8):
        o_ref[:, z * 896 : (z + 1) * 896] = jnp.concatenate(
            [p[:, z * 224 : (z + 1) * 224] for p in parts], 1
        ).astype(BF)


def arrange(where, here, mate, near, far):
    vmem = pl.BlockSpec(memory_space=pltpu.VMEM)
    return pl.pallas_call(
        arrange_body,
        in_specs=[pl.BlockSpec(memory_space=pltpu.SMEM)] + [vmem] * 4,
        out_specs=vmem,
        out_shape=jax.ShapeDtypeStruct((OWN, 7168), BF),
        name="arrange",
    )(where, here, mate, near, far)


def shards(
    queries,
    span_latent,
    span_rope,
    pool_latent,
    pool_rope,
    page_table,
    cache_len,
    span_len,
    kv_up,
    out_weight,
):
    zi, yl, xi, yh, ci = (lax.axis_index(a) for a in ("z", "yl", "x", "yh", "c"))
    group = zi * 2 + yl
    member = (xi * 2 + yh) * 2 + ci
    device = group * 16 + member
    slots = pool_latent.shape[0]
    pages = page_table.shape[1]
    swap_c = step("c", 2, 1)
    swap_yl = step("yl", 2, 1)
    swap_yh = step("yh", 2, 1)

    pair_latent, pair_rope = swap_yh(span_latent), swap_yh(span_rope)
    owners = page_table // slots
    slot_of = page_table % slots
    order = jnp.arange(pages, dtype=jnp.int32)
    marked = order[None, :] * slots + slot_of
    owned = owners == device
    low = jnp.min(jnp.where(owned, marked, pages * slots), axis=1)
    high = jnp.max(jnp.where(owned, marked, 0), axis=1)
    picked = jnp.stack([low % slots, high % slots], 1).reshape(32)
    sent_pages = pack(picked, pool_latent, pool_rope.reshape(slots, PAGE, ROPE))
    back = lax.all_to_all(sent_pages, ("z", "yl", "yh"), split_axis=0, concat_axis=0, tiled=True)
    fresh = pack_fresh(span_latent, span_rope, pair_latent, pair_rope)
    sent = split_queries(queries[0])
    turned = out_weight.T
    kept = lax.dynamic_slice_in_dim(turned, ci * 224, 224, 0)
    given = lax.dynamic_slice_in_dim(turned, (1 - ci) * 224, 224, 0)
    columns = jnp.concatenate([kept, swap_c(given)], 0)
    back, fresh, sent, columns = lax.optimization_barrier((back, fresh, sent, columns))
    weight = lax.all_gather(columns, "z", axis=0, tiled=False)
    mine = jnp.concatenate([back, fresh], 0)
    half = PIECE // 2
    left = step("x", 4, 1)(mine)
    right = step("x", 4, -1)(mine)
    exchanged = lax.all_to_all(sent, ("x", "yh", "c"), split_axis=0, concat_axis=0, tiled=True)
    q = exchanged.reshape(SPAN, HEADS_HERE * QHEAD)
    mine_c = swap_c(mine)
    far_a = step("x", 4, 1)(left[:half])
    far_b = step("x", 4, -1)(right[half:])
    left_c, right_c = swap_c(left), swap_c(right)
    pieces = [mine, left, right, far_a, far_b, mine_c, left_c, right_c, swap_c(far_a), swap_c(far_b)]

    my_table = lax.dynamic_index_in_dim(page_table, group, 0, keepdims=False)
    source = my_table // slots
    before = (source[None, :] == source[:, None]) & (order[None, :] < order[:, None])
    place = jnp.minimum(jnp.sum(before.astype(jnp.int32), axis=1), 1)
    from_group = source // 16
    from_member = source % 16

    def piece_index(of_member):
        apart = (of_member // 4 - xi) % 4
        number = jnp.where(apart == 0, 0, jnp.where(apart == 3, 1, jnp.where(apart == 1, 2, 3)))
        return (jnp.where(of_member % 2 == ci, 0, 4) + number) * PIECE

    block = piece_index(from_member) + from_group * 2 + (from_member // 2) % 2
    members = jnp.arange(32, dtype=jnp.int32) // 2
    block_new = piece_index(members) + 32 + jnp.where((members // 2) % 2 == yh, 0, 1)
    index = jnp.concatenate([block * 2 + place, block_new * 2 + jnp.arange(32, dtype=jnp.int32) % 2])

    lens = jnp.stack(
        [
            lax.dynamic_index_in_dim(cache_len, group, 0, keepdims=False),
            lax.dynamic_index_in_dim(span_len, group, 0, keepdims=False),
        ]
    )
    keys = assemble(index, pieces)
    own = [attend(half, lens, q, kv_up, keys) for half in range(2)]
    near = [swap_yl(x) for x in own]
    partial = project([*own, *near, *[swap_c(x) for x in own], *[swap_c(x) for x in near]], weight)
    shared = lax.all_to_all(partial, ("x", "yh"), split_axis=0, concat_axis=0, tiled=True)
    where = jnp.stack([yl, ci]).astype(jnp.int32)
    here, to_c, to_yl, to_both = total_parts(where, shared)
    from_both = lax.ppermute(to_both, ("yl", "c"), [(i, 3 - i) for i in range(4)])
    out = arrange(where, here, swap_c(to_c), swap_yl(to_yl), from_both)
    return out[None]


def solution(mesh):
    fine = Mesh(mesh.devices.reshape(8, 2, 4, 2, 2), ("z", "yl", "x", "yh", "c"))
    grp, head = ("z", "yl"), ("x", "yh", "c")
    return jax.shard_map(
        shards,
        mesh=fine,
        in_specs=(
            P(grp, head, None),
            P(grp, head, None),
            P(grp, head, None),
            P(grp + head, None, None),
            P(grp + head, None),
            P(),
            P(),
            P(),
            P(None, head),
            P(head, grp),
        ),
        out_specs=P(grp, head, None),
        check_vma=False,
    )
```

```python
import jax
import jax.numpy as jnp
from jax import lax
from jax.experimental import pallas as pl
from jax.experimental.pallas import tpu as pltpu
from jax.sharding import Mesh
from jax.sharding import PartitionSpec as P

LATENT = 512
ROPE = 64
NOPE = 128
VDIM = 128
PAGE = 8
QHEAD = NOPE + ROPE
HEADS_HERE = 8
SPAN = 192
OWN = 12
CTX = 2048
BF = jnp.bfloat16
F32 = jnp.float32
NEG = -1e30
LOG2E = 1.4426950408889634


def step(axis, count, by):
    def send(value):
        return lax.ppermute(value, axis, [(i, (i + by) % count) for i in range(count)])

    return send


def split_body(q_ref, o_ref):
    for part in range(16):
        o_ref[part] = q_ref[:, part * 1536 : (part + 1) * 1536]


def split_queries(q):
    vmem = pl.BlockSpec(memory_space=pltpu.VMEM)
    return pl.pallas_call(
        split_body,
        in_specs=[vmem],
        out_specs=vmem,
        out_shape=jax.ShapeDtypeStruct((16, OWN, 1536), BF),
        name="split_queries",
    )(q)


PIECE = 34
NT = (((1,), (1,)), ((), ()))
VMEM_BYTES = 56 * 1024 * 1024
ALLKEYS = CTX + 256
KWIDTH = LATENT + 2 * ROPE


def tiles_of(page):
    return jnp.concatenate([page[:, j * 128 : (j + 1) * 128] for j in range(4)], 0)


def pack_body(slot_ref, pool_ref, rope_ref, o_ref):
    def one(dest, carry):
        first = slot_ref[2 * dest]
        second = slot_ref[2 * dest + 1]
        tiles = jnp.concatenate([tiles_of(pool_ref[first]), tiles_of(pool_ref[second])], 0)
        rope = jnp.concatenate([rope_ref[first], rope_ref[second]], 1)
        o_ref[dest, :64] = tiles
        o_ref[dest, 64:] = rope
        return carry

    lax.fori_loop(0, 16, one, 0, unroll=2)


def pack(slots, pool, rope):
    vmem = pl.BlockSpec(memory_space=pltpu.VMEM)
    return pl.pallas_call(
        pack_body,
        in_specs=[pl.BlockSpec(memory_space=pltpu.SMEM), vmem, vmem],
        out_specs=vmem,
        out_shape=jax.ShapeDtypeStruct((16, 72, 128), BF),
        name="pack",
    )(slots, pool, rope)


def fresh_body(span_ref, span_rope_ref, pair_ref, pair_rope_ref, f_ref):
    gap = jnp.zeros((4, LATENT), F32)
    gap_rope = jnp.zeros((4, ROPE), F32)
    for k, (lat, rope) in enumerate(((span_ref, span_rope_ref), (pair_ref, pair_rope_ref))):
        x = jnp.concatenate([lat[0].astype(F32), gap], 0)
        y = jnp.concatenate([rope[0].astype(F32), gap_rope], 0)
        f_ref[k, :64] = jnp.concatenate([tiles_of(x[:8]), tiles_of(x[8:])], 0).astype(BF)
        f_ref[k, 64:] = jnp.concatenate([y[:8], y[8:]], 1).astype(BF)


def pack_fresh(*spans):
    vmem = pl.BlockSpec(memory_space=pltpu.VMEM)
    return pl.pallas_call(
        fresh_body,
        in_specs=[vmem] * 4,
        out_specs=vmem,
        out_shape=jax.ShapeDtypeStruct((2, 72, 128), BF),
        name="pack_fresh",
    )(*spans)


PLACES = ((0, 34), (34, 34), (68, 34), (102, 17), (119, 17))


def assemble_body(index_ref, *rest):
    pieces, keys, held, sems = rest[:10], rest[10], rest[11], rest[12]
    copies = []
    for n, piece in enumerate(pieces):
        start, size = PLACES[n % 5]
        start += 136 * (n // 5)
        copies.append(pltpu.make_async_copy(piece, held.at[start : start + size], sems.at[n]))
    for copy in copies:
        copy.start()
    for copy in copies:
        copy.wait()
    lane_half = lax.broadcasted_iota(jnp.int32, (8, 128), 1) // 64

    def pair(i, carry):
        lat, rope = [], []
        for k in range(2):
            at = index_ref[2 * i + k]
            block = at // 2
            place = at % 2
            lat.append(held[block, pl.ds(pl.multiple_of(place * 32, 32), 32), :])
            rope.append(jnp.where(lane_half == place, held[block, 64:72, :], jnp.zeros((), BF)))
        rows = pl.ds(pl.multiple_of(i * 16, 16), 16)
        for j in range(4):
            keys[rows, j * 128 : (j + 1) * 128] = jnp.concatenate(
                [lat[0][8 * j : 8 * j + 8], lat[1][8 * j : 8 * j + 8]], 0
            )
        keys[rows, LATENT:] = jnp.concatenate(rope, 0)
        return carry

    lax.fori_loop(0, ALLKEYS // 16, pair, 0, unroll=4)


def assemble(index, pieces):
    return pl.pallas_call(
        assemble_body,
        in_specs=[pl.BlockSpec(memory_space=pltpu.SMEM)] + [pl.BlockSpec(memory_space=pl.ANY)] * 10,
        out_specs=pl.BlockSpec(memory_space=pltpu.VMEM),
        out_shape=jax.ShapeDtypeStruct((ALLKEYS, KWIDTH), BF),
        scratch_shapes=[
            pltpu.VMEM((8 * PIECE, 72, 128), BF),
            pltpu.SemaphoreType.DMA((10,)),
        ],
        compiler_params=pltpu.CompilerParams(vmem_limit_bytes=24 * 1024 * 1024),
        cost_estimate=pl.CostEstimate(flops=0, bytes_accessed=16_000_000, transcendentals=0),
        name="assemble",
    )(index, *pieces)


def attend_body(lens_ref, q_ref, up_ref, keys, o_ref, qcat, causal):
    cached = lens_ref[0]
    appended = lens_ref[1]
    scale = LOG2E * (QHEAD**-0.5)

    @pl.when(pl.program_id(0) == 0)
    def prepare():
        row = lax.broadcasted_iota(jnp.int32, (SPAN, 256), 0)
        col = lax.broadcasted_iota(jnp.int32, (SPAN, 256), 1)
        token = col % 16
        seen = (token < OWN) & (col // 16 * OWN + token <= row)
        causal[...] = jnp.where(seen, 0.0, NEG).astype(F32)

    for h in range(2):
        rows = slice(h * SPAN, (h + 1) * SPAN)
        plain = q_ref[:, h * QHEAD : h * QHEAD + NOPE]
        key_up = up_ref[:, h * 256 : h * 256 + NOPE]
        qcat[rows, :LATENT] = lax.dot_general(plain, key_up, NT, preferred_element_type=F32).astype(BF)
        rope = q_ref[:, h * QHEAD + NOPE : (h + 1) * QHEAD]
        qcat[rows, LATENT:] = jnp.concatenate([rope, rope], 1)
    s = lax.dot_general(qcat[...], keys[...], NT, preferred_element_type=F32)
    at = lax.broadcasted_iota(jnp.int32, (1, CTX), 1)
    s = jnp.concatenate(
        [
            s[:, :CTX] + jnp.where(at < cached, 0.0, NEG),
            s[:, CTX:] + jnp.concatenate([causal[...], causal[...]], 0),
        ],
        1,
    )
    highest = jnp.max(s, axis=1, keepdims=True)
    p = jnp.exp2((s - highest) * scale)
    total = jnp.sum(p, axis=1, keepdims=True)
    mixed = jnp.dot(p.astype(BF), keys[:, :LATENT], preferred_element_type=F32)
    mixed = (mixed / total).astype(BF)
    live = lax.broadcasted_iota(jnp.int32, (SPAN, 1), 0) < appended
    for h in range(2):
        value_up = up_ref[:, h * 256 + NOPE : (h + 1) * 256]
        out = jnp.dot(mixed[h * SPAN : (h + 1) * SPAN], value_up, preferred_element_type=F32)
        o_ref[:, h * VDIM : (h + 1) * VDIM] = jnp.where(live, out, 0.0).astype(BF)


def attend(half, lens, q, up, keys):
    return pl.pallas_call(
        attend_body,
        grid_spec=pltpu.PrefetchScalarGridSpec(
            num_scalar_prefetch=1,
            grid=(2,),
            in_specs=[
                pl.BlockSpec((SPAN, 2 * QHEAD), lambda i, s: (0, 2 * half + i)),
                pl.BlockSpec((LATENT, 512), lambda i, s: (0, 2 * half + i)),
                pl.BlockSpec((ALLKEYS, KWIDTH), lambda i, s: (0, 0)),
            ],
            out_specs=pl.BlockSpec((SPAN, 256), lambda i, s: (0, i)),
            scratch_shapes=[
                pltpu.VMEM((2 * SPAN, KWIDTH), BF),
                pltpu.VMEM((SPAN, 256), F32),
            ],
        ),
        out_shape=jax.ShapeDtypeStruct((SPAN, 512), BF),
        compiler_params=pltpu.CompilerParams(vmem_limit_bytes=40 * 1024 * 1024),
        cost_estimate=pl.CostEstimate(
            flops=5_000_000_000, bytes_accessed=4_000_000, transcendentals=1_800_000
        ),
        name="attend",
    )(lens, q, up, keys)


def project_body(*refs):
    parts, w_ref, o_ref = refs[:8], refs[8], refs[9]
    own, near, mate, mate_near = (
        jnp.concatenate([parts[2 * k][...], parts[2 * k + 1][...]], 1) for k in range(4)
    )
    total = lax.dot_general(
        jnp.concatenate([own, near], 0),
        w_ref[:, :224].reshape(896, 1024),
        NT,
        preferred_element_type=F32,
    ) + lax.dot_general(
        jnp.concatenate([mate, mate_near], 0),
        w_ref[:, 224:].reshape(896, 1024),
        NT,
        preferred_element_type=F32,
    )
    for request in range(2):
        for place in range(8):
            at = request * SPAN + place * 24
            o_ref[place, request] = total[at : at + 24].astype(BF)


def project(parts, weight):
    return pl.pallas_call(
        project_body,
        grid=(2,),
        in_specs=[pl.BlockSpec((SPAN, 512), lambda i: (0, 0))] * 8
        + [pl.BlockSpec((4, 448, 1024), lambda i: (i, 0, 0))],
        out_specs=pl.BlockSpec((8, 2, 24, 896), lambda i: (0, 0, 0, i)),
        out_shape=jax.ShapeDtypeStruct((8, 2, 24, 1792), BF),
        compiler_params=pltpu.CompilerParams(vmem_limit_bytes=VMEM_BYTES),
        name="project",
    )(*parts, weight)


def arrange_body(where_ref, here_ref, c_ref, y_ref, both_ref, o_ref):
    yl, core = where_ref[0], where_ref[1]
    here, mate, near, far = (r[...].astype(F32) for r in (here_ref, c_ref, y_ref, both_ref))
    same = (jnp.where(core == 0, here, mate), jnp.where(core == 0, mate, here))
    other = (jnp.where(core == 0, near, far), jnp.where(core == 0, far, near))
    parts = [jnp.where(yl == 0, same[k], other[k]) for k in range(2)]
    parts += [jnp.where(yl == 0, other[k], same[k]) for k in range(2)]
    for z in range(8):
        o_ref[:, z * 896 : (z + 1) * 896] = jnp.concatenate(
            [p[:, z * 224 : (z + 1) * 224] for p in parts], 1
        ).astype(BF)


def arrange(where, here, mate, near, far):
    vmem = pl.BlockSpec(memory_space=pltpu.VMEM)
    return pl.pallas_call(
        arrange_body,
        in_specs=[pl.BlockSpec(memory_space=pltpu.SMEM)] + [vmem] * 4,
        out_specs=vmem,
        out_shape=jax.ShapeDtypeStruct((OWN, 7168), BF),
        name="arrange",
    )(where, here, mate, near, far)


def shards(
    queries,
    span_latent,
    span_rope,
    pool_latent,
    pool_rope,
    page_table,
    cache_len,
    span_len,
    kv_up,
    out_weight,
):
    zi, yl, xi, yh, ci = (lax.axis_index(a) for a in ("z", "yl", "x", "yh", "c"))
    group = zi * 2 + yl
    member = (xi * 2 + yh) * 2 + ci
    device = group * 16 + member
    slots = pool_latent.shape[0]
    pages = page_table.shape[1]
    swap_c = step("c", 2, 1)
    swap_yl = step("yl", 2, 1)
    swap_yh = step("yh", 2, 1)

    pair_latent, pair_rope = swap_yh(span_latent), swap_yh(span_rope)
    owners = page_table // slots
    slot_of = page_table % slots
    order = jnp.arange(pages, dtype=jnp.int32)
    marked = order[None, :] * slots + slot_of
    owned = owners == device
    low = jnp.min(jnp.where(owned, marked, pages * slots), axis=1)
    high = jnp.max(jnp.where(owned, marked, 0), axis=1)
    picked = jnp.stack([low % slots, high % slots], 1).reshape(32)
    sent_pages = pack(picked, pool_latent, pool_rope.reshape(slots, PAGE, ROPE))
    back = lax.all_to_all(sent_pages, ("z", "yl"), split_axis=0, concat_axis=0, tiled=True)
    fresh = pack_fresh(span_latent, span_rope, pair_latent, pair_rope)
    sent = split_queries(queries[0])
    lens = jnp.stack(
        [
            lax.dynamic_index_in_dim(cache_len, group, 0, keepdims=False),
            lax.dynamic_index_in_dim(span_len, group, 0, keepdims=False),
        ]
    )
    turned = out_weight.T
    kept = lax.dynamic_slice_in_dim(turned, ci * 224, 224, 0)
    given = lax.dynamic_slice_in_dim(turned, (1 - ci) * 224, 224, 0)
    columns = jnp.concatenate([kept, swap_c(given)], 0)
    back, fresh, sent, lens, columns = lax.optimization_barrier((back, fresh, sent, lens, columns))
    weight = lax.all_gather(columns, "z", axis=0, tiled=False)
    mine = jnp.concatenate([back, swap_yh(back), fresh], 0)
    half = PIECE // 2
    left = step("x", 4, 1)(mine)
    right = step("x", 4, -1)(mine)
    exchanged = lax.all_to_all(sent, ("x", "yh", "c"), split_axis=0, concat_axis=0, tiled=True)
    mine_c = swap_c(mine)
    far_a = step("x", 4, 1)(left[:half])
    far_b = step("x", 4, -1)(right[half:])
    left_c, right_c = swap_c(left), swap_c(right)
    pieces = [mine, left, right, far_a, far_b, mine_c, left_c, right_c, swap_c(far_a), swap_c(far_b)]

    my_table = lax.dynamic_index_in_dim(page_table, group, 0, keepdims=False)
    source = my_table // slots
    before = (source[None, :] == source[:, None]) & (order[None, :] < order[:, None])
    place = jnp.minimum(jnp.sum(before.astype(jnp.int32), axis=1), 1)
    from_group = source // 16
    from_member = source % 16

    def piece_index(of_member):
        apart = (of_member // 4 - xi) % 4
        number = jnp.where(apart == 0, 0, jnp.where(apart == 3, 1, jnp.where(apart == 1, 2, 3)))
        return (jnp.where(of_member % 2 == ci, 0, 4) + number) * PIECE

    block = piece_index(from_member) + from_group + jnp.where((from_member // 2) % 2 == yh, 0, 16)
    members = jnp.arange(32, dtype=jnp.int32) // 2
    block_new = piece_index(members) + 32 + jnp.where((members // 2) % 2 == yh, 0, 1)
    index = jnp.concatenate([block * 2 + place, block_new * 2 + jnp.arange(32, dtype=jnp.int32) % 2])

    keys = assemble(index, pieces)
    exchanged, keys = lax.optimization_barrier((exchanged, keys))
    q = exchanged.reshape(SPAN, HEADS_HERE * QHEAD)
    own = [attend(half, lens, q, kv_up, keys) for half in range(2)]
    near = [swap_yl(x) for x in own]
    partial = project([*own, *near, *[swap_c(x) for x in own], *[swap_c(x) for x in near]], weight)
    shared = lax.all_to_all(partial, ("x", "yh"), split_axis=0, concat_axis=0, tiled=True)
    where = jnp.stack([yl, ci]).astype(jnp.int32)
    summed = jnp.sum(shared.astype(F32), axis=0).astype(BF).reshape(2, 2, OWN, 1792)
    own_rows = lax.dynamic_index_in_dim(summed, ci, 1, keepdims=False)
    mate_rows = lax.dynamic_index_in_dim(summed, 1 - ci, 1, keepdims=False)
    here, to_c, to_yl, to_both = own_rows[0], mate_rows[0], own_rows[1], mate_rows[1]
    from_both = lax.ppermute(to_both, ("yl", "c"), [(i, 3 - i) for i in range(4)])
    out = arrange(where, here, swap_c(to_c), swap_yl(to_yl), from_both)
    return out[None]


def solution(mesh):
    fine = Mesh(mesh.devices.reshape(8, 2, 4, 2, 2), ("z", "yl", "x", "yh", "c"))
    grp, head = ("z", "yl"), ("x", "yh", "c")
    return jax.shard_map(
        shards,
        mesh=fine,
        in_specs=(
            P(grp, head, None),
            P(grp, head, None),
            P(grp, head, None),
            P(grp + head, None, None),
            P(grp + head, None),
            P(),
            P(),
            P(),
            P(None, head),
            P(head, grp),
        ),
        out_specs=P(grp, head, None),
        check_vma=False,
    )
```

```python
import jax
import jax.numpy as jnp
from jax import lax
from jax.experimental import pallas as pl
from jax.experimental.pallas import tpu as pltpu
from jax.sharding import Mesh
from jax.sharding import PartitionSpec as P

LATENT = 512
ROPE = 64
NOPE = 128
VDIM = 128
PAGE = 8
QHEAD = NOPE + ROPE
HEADS_HERE = 8
SPAN = 192
OWN = 12
CTX = 2048
BF = jnp.bfloat16
F32 = jnp.float32
NEG = -1e30
LOG2E = 1.4426950408889634


def step(axis, count, by):
    def send(value):
        return lax.ppermute(value, axis, [(i, (i + by) % count) for i in range(count)])

    return send


def split_body(q_ref, o_ref):
    for part in range(16):
        o_ref[part] = q_ref[:, part * 1536 : (part + 1) * 1536]


def split_queries(q):
    vmem = pl.BlockSpec(memory_space=pltpu.VMEM)
    return pl.pallas_call(
        split_body,
        in_specs=[vmem],
        out_specs=vmem,
        out_shape=jax.ShapeDtypeStruct((16, OWN, 1536), BF),
        name="split_queries",
    )(q)


PIECE = 34
NT = (((1,), (1,)), ((), ()))
VMEM_BYTES = 56 * 1024 * 1024
ALLKEYS = CTX + 256
KWIDTH = LATENT + 2 * ROPE


def tiles_of(page):
    return jnp.concatenate([page[:, j * 128 : (j + 1) * 128] for j in range(4)], 0)


def pack_body(slot_ref, pool_ref, rope_ref, o_ref):
    def one(dest, carry):
        first = slot_ref[2 * dest]
        second = slot_ref[2 * dest + 1]
        tiles = jnp.concatenate([tiles_of(pool_ref[first]), tiles_of(pool_ref[second])], 0)
        rope = jnp.concatenate([rope_ref[first], rope_ref[second]], 1)
        o_ref[dest, :64] = tiles
        o_ref[dest, 64:] = rope
        return carry

    lax.fori_loop(0, 16, one, 0, unroll=2)


def pack(slots, pool, rope):
    vmem = pl.BlockSpec(memory_space=pltpu.VMEM)
    return pl.pallas_call(
        pack_body,
        in_specs=[pl.BlockSpec(memory_space=pltpu.SMEM), vmem, vmem],
        out_specs=vmem,
        out_shape=jax.ShapeDtypeStruct((16, 72, 128), BF),
        name="pack",
    )(slots, pool, rope)


def fresh_body(span_ref, span_rope_ref, pair_ref, pair_rope_ref, f_ref):
    gap = jnp.zeros((4, LATENT), F32)
    gap_rope = jnp.zeros((4, ROPE), F32)
    for k, (lat, rope) in enumerate(((span_ref, span_rope_ref), (pair_ref, pair_rope_ref))):
        x = jnp.concatenate([lat[0].astype(F32), gap], 0)
        y = jnp.concatenate([rope[0].astype(F32), gap_rope], 0)
        f_ref[k, :64] = jnp.concatenate([tiles_of(x[:8]), tiles_of(x[8:])], 0).astype(BF)
        f_ref[k, 64:] = jnp.concatenate([y[:8], y[8:]], 1).astype(BF)


def pack_fresh(*spans):
    vmem = pl.BlockSpec(memory_space=pltpu.VMEM)
    return pl.pallas_call(
        fresh_body,
        in_specs=[vmem] * 4,
        out_specs=vmem,
        out_shape=jax.ShapeDtypeStruct((2, 72, 128), BF),
        name="pack_fresh",
    )(*spans)


PLACES = ((0, 34), (34, 34), (68, 34), (102, 17), (119, 17))


def assemble_body(index_ref, *rest):
    pieces, keys, held, sems = rest[:10], rest[10], rest[11], rest[12]
    copies = []
    for n, piece in enumerate(pieces):
        start, size = PLACES[n % 5]
        start += 136 * (n // 5)
        copies.append(pltpu.make_async_copy(piece, held.at[start : start + size], sems.at[n]))
    for copy in copies:
        copy.start()
    for copy in copies:
        copy.wait()
    lane_half = lax.broadcasted_iota(jnp.int32, (8, 128), 1) // 64

    def pair(i, carry):
        lat, rope = [], []
        for k in range(2):
            at = index_ref[2 * i + k]
            block = at // 2
            place = at % 2
            lat.append(held[block, pl.ds(pl.multiple_of(place * 32, 32), 32), :])
            rope.append(jnp.where(lane_half == place, held[block, 64:72, :], jnp.zeros((), BF)))
        rows = pl.ds(pl.multiple_of(i * 16, 16), 16)
        for j in range(4):
            keys[rows, j * 128 : (j + 1) * 128] = jnp.concatenate(
                [lat[0][8 * j : 8 * j + 8], lat[1][8 * j : 8 * j + 8]], 0
            )
        keys[rows, LATENT:] = jnp.concatenate(rope, 0)
        return carry

    lax.fori_loop(0, ALLKEYS // 16, pair, 0, unroll=4)


def assemble(index, pieces):
    return pl.pallas_call(
        assemble_body,
        in_specs=[pl.BlockSpec(memory_space=pltpu.SMEM)] + [pl.BlockSpec(memory_space=pl.ANY)] * 10,
        out_specs=pl.BlockSpec(memory_space=pltpu.VMEM),
        out_shape=jax.ShapeDtypeStruct((ALLKEYS, KWIDTH), BF),
        scratch_shapes=[
            pltpu.VMEM((8 * PIECE, 72, 128), BF),
            pltpu.SemaphoreType.DMA((10,)),
        ],
        compiler_params=pltpu.CompilerParams(vmem_limit_bytes=24 * 1024 * 1024),
        cost_estimate=pl.CostEstimate(flops=0, bytes_accessed=16_000_000, transcendentals=0),
        name="assemble",
    )(index, *pieces)


def attend_body(lens_ref, q_ref, up_ref, keys, o_ref, qcat, causal):
    cached = lens_ref[0]
    appended = lens_ref[1]
    scale = LOG2E * (QHEAD**-0.5)

    @pl.when(pl.program_id(0) == 0)
    def prepare():
        row = lax.broadcasted_iota(jnp.int32, (SPAN, 256), 0)
        col = lax.broadcasted_iota(jnp.int32, (SPAN, 256), 1)
        token = col % 16
        seen = (token < OWN) & (col // 16 * OWN + token <= row)
        causal[...] = jnp.where(seen, 0.0, NEG).astype(F32)

    for h in range(2):
        rows = slice(h * SPAN, (h + 1) * SPAN)
        plain = q_ref[:, h * QHEAD : h * QHEAD + NOPE]
        key_up = up_ref[:, h * 256 : h * 256 + NOPE]
        qcat[rows, :LATENT] = lax.dot_general(plain, key_up, NT, preferred_element_type=F32).astype(BF)
        rope = q_ref[:, h * QHEAD + NOPE : (h + 1) * QHEAD]
        qcat[rows, LATENT:] = jnp.concatenate([rope, rope], 1)
    s = lax.dot_general(qcat[...], keys[...], NT, preferred_element_type=F32)
    at = lax.broadcasted_iota(jnp.int32, (1, CTX), 1)
    s = jnp.concatenate(
        [
            s[:, :CTX] + jnp.where(at < cached, 0.0, NEG),
            s[:, CTX:] + jnp.concatenate([causal[...], causal[...]], 0),
        ],
        1,
    )
    highest = jnp.max(s, axis=1, keepdims=True)
    p = jnp.exp2((s - highest) * scale)
    total = jnp.sum(p, axis=1, keepdims=True)
    mixed = jnp.dot(p.astype(BF), keys[:, :LATENT], preferred_element_type=F32)
    mixed = (mixed / total).astype(BF)
    live = lax.broadcasted_iota(jnp.int32, (SPAN, 1), 0) < appended
    for h in range(2):
        value_up = up_ref[:, h * 256 + NOPE : (h + 1) * 256]
        out = jnp.dot(mixed[h * SPAN : (h + 1) * SPAN], value_up, preferred_element_type=F32)
        o_ref[:, h * VDIM : (h + 1) * VDIM] = jnp.where(live, out, 0.0).astype(BF)


def attend(half, lens, q, up, keys):
    return pl.pallas_call(
        attend_body,
        grid_spec=pltpu.PrefetchScalarGridSpec(
            num_scalar_prefetch=1,
            grid=(2,),
            in_specs=[
                pl.BlockSpec((SPAN, 2 * QHEAD), lambda i, s: (0, 2 * half + i)),
                pl.BlockSpec((LATENT, 512), lambda i, s: (0, 2 * half + i)),
                pl.BlockSpec((ALLKEYS, KWIDTH), lambda i, s: (0, 0)),
            ],
            out_specs=pl.BlockSpec((SPAN, 256), lambda i, s: (0, i)),
            scratch_shapes=[
                pltpu.VMEM((2 * SPAN, KWIDTH), BF),
                pltpu.VMEM((SPAN, 256), F32),
            ],
        ),
        out_shape=jax.ShapeDtypeStruct((SPAN, 512), BF),
        compiler_params=pltpu.CompilerParams(vmem_limit_bytes=40 * 1024 * 1024),
        cost_estimate=pl.CostEstimate(
            flops=5_000_000_000, bytes_accessed=4_000_000, transcendentals=1_800_000
        ),
        name="attend",
    )(lens, q, up, keys)


def project_body(*refs):
    parts, w_ref, o_ref = refs[:8], refs[8], refs[9]
    own, near, mate, mate_near = (
        jnp.concatenate([parts[2 * k][...], parts[2 * k + 1][...]], 1) for k in range(4)
    )
    total = lax.dot_general(
        jnp.concatenate([own, near], 0),
        w_ref[:, :224].reshape(896, 1024),
        NT,
        preferred_element_type=F32,
    ) + lax.dot_general(
        jnp.concatenate([mate, mate_near], 0),
        w_ref[:, 224:].reshape(896, 1024),
        NT,
        preferred_element_type=F32,
    )
    for request in range(2):
        for place in range(8):
            at = request * SPAN + place * 24
            o_ref[place, request] = total[at : at + 24].astype(BF)


def project(parts, weight):
    return pl.pallas_call(
        project_body,
        grid=(2,),
        in_specs=[pl.BlockSpec((SPAN, 512), lambda i: (0, 0))] * 8
        + [pl.BlockSpec((4, 448, 1024), lambda i: (i, 0, 0))],
        out_specs=pl.BlockSpec((8, 2, 24, 896), lambda i: (0, 0, 0, i)),
        out_shape=jax.ShapeDtypeStruct((8, 2, 24, 1792), BF),
        compiler_params=pltpu.CompilerParams(vmem_limit_bytes=VMEM_BYTES),
        name="project",
    )(*parts, weight)


def arrange_body(where_ref, here_ref, c_ref, y_ref, both_ref, o_ref):
    yl, core = where_ref[0], where_ref[1]
    here, mate, near, far = (r[...].astype(F32) for r in (here_ref, c_ref, y_ref, both_ref))
    same = (jnp.where(core == 0, here, mate), jnp.where(core == 0, mate, here))
    other = (jnp.where(core == 0, near, far), jnp.where(core == 0, far, near))
    parts = [jnp.where(yl == 0, same[k], other[k]) for k in range(2)]
    parts += [jnp.where(yl == 0, other[k], same[k]) for k in range(2)]
    for z in range(8):
        o_ref[:, z * 896 : (z + 1) * 896] = jnp.concatenate(
            [p[:, z * 224 : (z + 1) * 224] for p in parts], 1
        ).astype(BF)


def arrange(where, here, mate, near, far):
    vmem = pl.BlockSpec(memory_space=pltpu.VMEM)
    return pl.pallas_call(
        arrange_body,
        in_specs=[pl.BlockSpec(memory_space=pltpu.SMEM)] + [vmem] * 4,
        out_specs=vmem,
        out_shape=jax.ShapeDtypeStruct((OWN, 7168), BF),
        name="arrange",
    )(where, here, mate, near, far)


def shards(
    queries,
    span_latent,
    span_rope,
    pool_latent,
    pool_rope,
    page_table,
    cache_len,
    span_len,
    kv_up,
    out_weight,
):
    zi, yl, xi, yh, ci = (lax.axis_index(a) for a in ("z", "yl", "x", "yh", "c"))
    group = zi * 2 + yl
    member = (xi * 2 + yh) * 2 + ci
    device = group * 16 + member
    slots = pool_latent.shape[0]
    pages = page_table.shape[1]
    swap_c = step("c", 2, 1)
    swap_yl = step("yl", 2, 1)
    swap_yh = step("yh", 2, 1)

    pair_latent, pair_rope = swap_yh(span_latent), swap_yh(span_rope)
    owners = page_table // slots
    slot_of = page_table % slots
    order = jnp.arange(pages, dtype=jnp.int32)
    marked = order[None, :] * slots + slot_of
    owned = owners == device
    low = jnp.min(jnp.where(owned, marked, pages * slots), axis=1)
    high = jnp.max(jnp.where(owned, marked, 0), axis=1)
    picked = jnp.stack([low % slots, high % slots], 1).reshape(32)
    sent_pages = pack(picked, pool_latent, pool_rope.reshape(slots, PAGE, ROPE))
    out_weight, sent_pages = lax.optimization_barrier((out_weight, sent_pages))
    turned = out_weight.T
    kept = lax.dynamic_slice_in_dim(turned, ci * 224, 224, 0)
    given = lax.dynamic_slice_in_dim(turned, (1 - ci) * 224, 224, 0)
    columns = jnp.concatenate([kept, swap_c(given)], 0)
    back = lax.all_to_all(sent_pages, ("z", "yl"), split_axis=0, concat_axis=0, tiled=True)
    fresh = pack_fresh(span_latent, span_rope, pair_latent, pair_rope)
    sent = split_queries(queries[0])
    lens = jnp.stack(
        [
            lax.dynamic_index_in_dim(cache_len, group, 0, keepdims=False),
            lax.dynamic_index_in_dim(span_len, group, 0, keepdims=False),
        ]
    )
    back, columns = lax.optimization_barrier((back, columns))
    weight = lax.all_gather(columns, "z", axis=0, tiled=False)
    mine = jnp.concatenate([back, swap_yh(back), fresh], 0)
    half = PIECE // 2
    left = step("x", 4, 1)(mine)
    right = step("x", 4, -1)(mine)
    exchanged = lax.all_to_all(sent, ("x", "yh", "c"), split_axis=0, concat_axis=0, tiled=True)
    mine_c = swap_c(mine)
    far_a = step("x", 4, 1)(left[:half])
    far_b = step("x", 4, -1)(right[half:])
    left_c, right_c = swap_c(left), swap_c(right)
    pieces = [mine, left, right, far_a, far_b, mine_c, left_c, right_c, swap_c(far_a), swap_c(far_b)]

    my_table = lax.dynamic_index_in_dim(page_table, group, 0, keepdims=False)
    source = my_table // slots
    before = (source[None, :] == source[:, None]) & (order[None, :] < order[:, None])
    place = jnp.minimum(jnp.sum(before.astype(jnp.int32), axis=1), 1)
    from_group = source // 16
    from_member = source % 16

    def piece_index(of_member):
        apart = (of_member // 4 - xi) % 4
        number = jnp.where(apart == 0, 0, jnp.where(apart == 3, 1, jnp.where(apart == 1, 2, 3)))
        return (jnp.where(of_member % 2 == ci, 0, 4) + number) * PIECE

    block = piece_index(from_member) + from_group + jnp.where((from_member // 2) % 2 == yh, 0, 16)
    members = jnp.arange(32, dtype=jnp.int32) // 2
    block_new = piece_index(members) + 32 + jnp.where((members // 2) % 2 == yh, 0, 1)
    index = jnp.concatenate([block * 2 + place, block_new * 2 + jnp.arange(32, dtype=jnp.int32) % 2])

    keys = assemble(index, pieces)
    exchanged, keys = lax.optimization_barrier((exchanged, keys))
    q = exchanged.reshape(SPAN, HEADS_HERE * QHEAD)
    own = [attend(half, lens, q, kv_up, keys) for half in range(2)]
    near = [swap_yl(x) for x in own]
    partial = project([*own, *near, *[swap_c(x) for x in own], *[swap_c(x) for x in near]], weight)
    shared = lax.all_to_all(partial, ("x", "yh"), split_axis=0, concat_axis=0, tiled=True)
    where = jnp.stack([yl, ci]).astype(jnp.int32)
    summed = jnp.sum(shared.astype(F32), axis=0).astype(BF).reshape(2, 2, OWN, 1792)
    own_rows = lax.dynamic_index_in_dim(summed, ci, 1, keepdims=False)
    mate_rows = lax.dynamic_index_in_dim(summed, 1 - ci, 1, keepdims=False)
    here, to_c, to_yl, to_both = own_rows[0], mate_rows[0], own_rows[1], mate_rows[1]
    from_both = lax.ppermute(to_both, ("yl", "c"), [(i, 3 - i) for i in range(4)])
    out = arrange(where, here, swap_c(to_c), swap_yl(to_yl), from_both)
    return out[None]


def solution(mesh):
    fine = Mesh(mesh.devices.reshape(8, 2, 4, 2, 2), ("z", "yl", "x", "yh", "c"))
    grp, head = ("z", "yl"), ("x", "yh", "c")
    return jax.shard_map(
        shards,
        mesh=fine,
        in_specs=(
            P(grp, head, None),
            P(grp, head, None),
            P(grp, head, None),
            P(grp + head, None, None),
            P(grp + head, None),
            P(),
            P(),
            P(),
            P(None, head),
            P(head, grp),
        ),
        out_specs=P(grp, head, None),
        check_vma=False,
    )
```

```python
import jax
import jax.numpy as jnp
from jax import lax
from jax.experimental import pallas as pl
from jax.experimental.pallas import tpu as pltpu
from jax.sharding import Mesh
from jax.sharding import PartitionSpec as P

LATENT = 512
ROPE = 64
NOPE = 128
VDIM = 128
PAGE = 8
QHEAD = NOPE + ROPE
HEADS_HERE = 8
SPAN = 192
OWN = 12
CTX = 2048
BF = jnp.bfloat16
F32 = jnp.float32
NEG = -1e30
LOG2E = 1.4426950408889634


def step(axis, count, by):
    def send(value):
        return lax.ppermute(value, axis, [(i, (i + by) % count) for i in range(count)])

    return send


def split_body(q_ref, o_ref):
    for part in range(16):
        o_ref[part] = q_ref[:, part * 1536 : (part + 1) * 1536]


def split_queries(q):
    vmem = pl.BlockSpec(memory_space=pltpu.VMEM)
    return pl.pallas_call(
        split_body,
        in_specs=[vmem],
        out_specs=vmem,
        out_shape=jax.ShapeDtypeStruct((16, OWN, 1536), BF),
        name="split_queries",
    )(q)


PIECE = 34
NT = (((1,), (1,)), ((), ()))
VMEM_BYTES = 56 * 1024 * 1024
ALLKEYS = CTX + 256
KWIDTH = LATENT + 2 * ROPE


def tiles_of(page):
    return jnp.concatenate([page[:, j * 128 : (j + 1) * 128] for j in range(4)], 0)


def pack_body(slot_ref, pool_ref, rope_ref, o_ref):
    def one(dest, carry):
        first = slot_ref[2 * dest]
        second = slot_ref[2 * dest + 1]
        tiles = jnp.concatenate([tiles_of(pool_ref[first]), tiles_of(pool_ref[second])], 0)
        rope = jnp.concatenate([rope_ref[first], rope_ref[second]], 1)
        o_ref[dest, :64] = tiles
        o_ref[dest, 64:] = rope
        return carry

    lax.fori_loop(0, 16, one, 0, unroll=2)


def pack(slots, pool, rope):
    vmem = pl.BlockSpec(memory_space=pltpu.VMEM)
    return pl.pallas_call(
        pack_body,
        in_specs=[pl.BlockSpec(memory_space=pltpu.SMEM), vmem, vmem],
        out_specs=vmem,
        out_shape=jax.ShapeDtypeStruct((16, 72, 128), BF),
        name="pack",
    )(slots, pool, rope)


def fresh_body(span_ref, span_rope_ref, pair_ref, pair_rope_ref, f_ref):
    gap = jnp.zeros((4, LATENT), F32)
    gap_rope = jnp.zeros((4, ROPE), F32)
    for k, (lat, rope) in enumerate(((span_ref, span_rope_ref), (pair_ref, pair_rope_ref))):
        x = jnp.concatenate([lat[0].astype(F32), gap], 0)
        y = jnp.concatenate([rope[0].astype(F32), gap_rope], 0)
        f_ref[k, :64] = jnp.concatenate([tiles_of(x[:8]), tiles_of(x[8:])], 0).astype(BF)
        f_ref[k, 64:] = jnp.concatenate([y[:8], y[8:]], 1).astype(BF)


def pack_fresh(*spans):
    vmem = pl.BlockSpec(memory_space=pltpu.VMEM)
    return pl.pallas_call(
        fresh_body,
        in_specs=[vmem] * 4,
        out_specs=vmem,
        out_shape=jax.ShapeDtypeStruct((2, 72, 128), BF),
        name="pack_fresh",
    )(*spans)


PLACES = ((0, 34), (34, 34), (68, 34), (102, 17), (119, 17))


def assemble_body(index_ref, *rest):
    pieces, keys, held, sems = rest[:10], rest[10], rest[11], rest[12]
    copies = []
    for n, piece in enumerate(pieces):
        start, size = PLACES[n % 5]
        start += 136 * (n // 5)
        copies.append(pltpu.make_async_copy(piece, held.at[start : start + size], sems.at[n]))
    for copy in copies:
        copy.start()
    for copy in copies:
        copy.wait()
    lane_half = lax.broadcasted_iota(jnp.int32, (8, 128), 1) // 64

    def pair(i, carry):
        lat, rope = [], []
        for k in range(2):
            at = index_ref[2 * i + k]
            block = at // 2
            place = at % 2
            lat.append(held[block, pl.ds(pl.multiple_of(place * 32, 32), 32), :])
            rope.append(jnp.where(lane_half == place, held[block, 64:72, :], jnp.zeros((), BF)))
        rows = pl.ds(pl.multiple_of(i * 16, 16), 16)
        for j in range(4):
            keys[rows, j * 128 : (j + 1) * 128] = jnp.concatenate(
                [lat[0][8 * j : 8 * j + 8], lat[1][8 * j : 8 * j + 8]], 0
            )
        keys[rows, LATENT:] = jnp.concatenate(rope, 0)
        return carry

    lax.fori_loop(0, ALLKEYS // 16, pair, 0, unroll=4)


def assemble(index, pieces):
    return pl.pallas_call(
        assemble_body,
        in_specs=[pl.BlockSpec(memory_space=pltpu.SMEM)] + [pl.BlockSpec(memory_space=pl.ANY)] * 10,
        out_specs=pl.BlockSpec(memory_space=pltpu.VMEM),
        out_shape=jax.ShapeDtypeStruct((ALLKEYS, KWIDTH), BF),
        scratch_shapes=[
            pltpu.VMEM((8 * PIECE, 72, 128), BF),
            pltpu.SemaphoreType.DMA((10,)),
        ],
        compiler_params=pltpu.CompilerParams(vmem_limit_bytes=24 * 1024 * 1024),
        cost_estimate=pl.CostEstimate(flops=0, bytes_accessed=16_000_000, transcendentals=0),
        name="assemble",
    )(index, *pieces)


def attend_body(lens_ref, q_ref, up_ref, keys, o_ref, qcat, causal):
    cached = lens_ref[0]
    appended = lens_ref[1]
    scale = LOG2E * (QHEAD**-0.5)

    @pl.when(pl.program_id(0) == 0)
    def prepare():
        row = lax.broadcasted_iota(jnp.int32, (SPAN, 256), 0)
        col = lax.broadcasted_iota(jnp.int32, (SPAN, 256), 1)
        token = col % 16
        seen = (token < OWN) & (col // 16 * OWN + token <= row)
        causal[...] = jnp.where(seen, 0.0, NEG).astype(F32)

    for h in range(2):
        rows = slice(h * SPAN, (h + 1) * SPAN)
        plain = q_ref[:, h * QHEAD : h * QHEAD + NOPE]
        key_up = up_ref[:, h * 256 : h * 256 + NOPE]
        qcat[rows, :LATENT] = lax.dot_general(plain, key_up, NT, preferred_element_type=F32).astype(BF)
        rope = q_ref[:, h * QHEAD + NOPE : (h + 1) * QHEAD]
        qcat[rows, LATENT:] = jnp.concatenate([rope, rope], 1)
    s = lax.dot_general(qcat[...], keys[...], NT, preferred_element_type=F32)
    at = lax.broadcasted_iota(jnp.int32, (1, CTX), 1)
    s = jnp.concatenate(
        [
            s[:, :CTX] + jnp.where(at < cached, 0.0, NEG),
            s[:, CTX:] + jnp.concatenate([causal[...], causal[...]], 0),
        ],
        1,
    )
    highest = jnp.max(s, axis=1, keepdims=True)
    p = jnp.exp2((s - highest) * scale)
    total = jnp.sum(p, axis=1, keepdims=True)
    mixed = jnp.dot(p.astype(BF), keys[:, :LATENT], preferred_element_type=F32)
    mixed = (mixed / total).astype(BF)
    live = lax.broadcasted_iota(jnp.int32, (SPAN, 1), 0) < appended
    for h in range(2):
        value_up = up_ref[:, h * 256 + NOPE : (h + 1) * 256]
        out = jnp.dot(mixed[h * SPAN : (h + 1) * SPAN], value_up, preferred_element_type=F32)
        o_ref[:, h * VDIM : (h + 1) * VDIM] = jnp.where(live, out, 0.0).astype(BF)


def attend(half, lens, q, up, keys):
    return pl.pallas_call(
        attend_body,
        grid_spec=pltpu.PrefetchScalarGridSpec(
            num_scalar_prefetch=1,
            grid=(2,),
            in_specs=[
                pl.BlockSpec((SPAN, 2 * QHEAD), lambda i, s: (0, 2 * half + i)),
                pl.BlockSpec((LATENT, 512), lambda i, s: (0, 2 * half + i)),
                pl.BlockSpec((ALLKEYS, KWIDTH), lambda i, s: (0, 0)),
            ],
            out_specs=pl.BlockSpec((SPAN, 256), lambda i, s: (0, i)),
            scratch_shapes=[
                pltpu.VMEM((2 * SPAN, KWIDTH), BF),
                pltpu.VMEM((SPAN, 256), F32),
            ],
        ),
        out_shape=jax.ShapeDtypeStruct((SPAN, 512), BF),
        compiler_params=pltpu.CompilerParams(vmem_limit_bytes=40 * 1024 * 1024),
        cost_estimate=pl.CostEstimate(
            flops=5_000_000_000, bytes_accessed=4_000_000, transcendentals=1_800_000
        ),
        name="attend",
    )(lens, q, up, keys)


def project_body(*refs):
    parts, w_ref, o_ref = refs[:8], refs[8], refs[9]
    own, near, mate, mate_near = (
        jnp.concatenate([parts[2 * k][...], parts[2 * k + 1][...]], 1) for k in range(4)
    )
    total = lax.dot_general(
        jnp.concatenate([own, near], 0),
        w_ref[:, :224].reshape(896, 1024),
        NT,
        preferred_element_type=F32,
    ) + lax.dot_general(
        jnp.concatenate([mate, mate_near], 0),
        w_ref[:, 224:].reshape(896, 1024),
        NT,
        preferred_element_type=F32,
    )
    for request in range(2):
        for place in range(8):
            at = request * SPAN + place * 24
            o_ref[place, request] = total[at : at + 24].astype(BF)


def project(parts, weight):
    return pl.pallas_call(
        project_body,
        grid=(2,),
        in_specs=[pl.BlockSpec((SPAN, 512), lambda i: (0, 0))] * 8
        + [pl.BlockSpec((4, 448, 1024), lambda i: (i, 0, 0))],
        out_specs=pl.BlockSpec((8, 2, 24, 896), lambda i: (0, 0, 0, i)),
        out_shape=jax.ShapeDtypeStruct((8, 2, 24, 1792), BF),
        compiler_params=pltpu.CompilerParams(vmem_limit_bytes=VMEM_BYTES),
        name="project",
    )(*parts, weight)


def arrange_body(where_ref, here_ref, c_ref, y_ref, both_ref, o_ref):
    yl, core = where_ref[0], where_ref[1]
    here, mate, near, far = (r[...].astype(F32) for r in (here_ref, c_ref, y_ref, both_ref))
    same = (jnp.where(core == 0, here, mate), jnp.where(core == 0, mate, here))
    other = (jnp.where(core == 0, near, far), jnp.where(core == 0, far, near))
    parts = [jnp.where(yl == 0, same[k], other[k]) for k in range(2)]
    parts += [jnp.where(yl == 0, other[k], same[k]) for k in range(2)]
    for z in range(8):
        o_ref[:, z * 896 : (z + 1) * 896] = jnp.concatenate(
            [p[:, z * 224 : (z + 1) * 224] for p in parts], 1
        ).astype(BF)


def arrange(where, here, mate, near, far):
    vmem = pl.BlockSpec(memory_space=pltpu.VMEM)
    return pl.pallas_call(
        arrange_body,
        in_specs=[pl.BlockSpec(memory_space=pltpu.SMEM)] + [vmem] * 4,
        out_specs=vmem,
        out_shape=jax.ShapeDtypeStruct((OWN, 7168), BF),
        name="arrange",
    )(where, here, mate, near, far)


def shards(
    queries,
    span_latent,
    span_rope,
    pool_latent,
    pool_rope,
    page_table,
    cache_len,
    span_len,
    kv_up,
    out_weight,
):
    zi, yl, xi, yh, ci = (lax.axis_index(a) for a in ("z", "yl", "x", "yh", "c"))
    group = zi * 2 + yl
    member = (xi * 2 + yh) * 2 + ci
    device = group * 16 + member
    slots = pool_latent.shape[0]
    pages = page_table.shape[1]
    swap_c = step("c", 2, 1)
    swap_yl = step("yl", 2, 1)
    swap_yh = step("yh", 2, 1)

    pair_latent, pair_rope = swap_yh(span_latent), swap_yh(span_rope)
    owners = page_table // slots
    slot_of = page_table % slots
    order = jnp.arange(pages, dtype=jnp.int32)
    marked = order[None, :] * slots + slot_of
    owned = owners == device
    low = jnp.min(jnp.where(owned, marked, pages * slots), axis=1)
    high = jnp.max(jnp.where(owned, marked, 0), axis=1)
    picked = jnp.stack([low % slots, high % slots], 1).reshape(32)
    sent_pages = pack(picked, pool_latent, pool_rope.reshape(slots, PAGE, ROPE))
    out_weight, sent_pages = lax.optimization_barrier((out_weight, sent_pages))
    turned = out_weight.T
    kept = lax.dynamic_slice_in_dim(turned, ci * 224, 224, 0)
    given = lax.dynamic_slice_in_dim(turned, (1 - ci) * 224, 224, 0)
    columns = jnp.concatenate([kept, swap_c(given)], 0)
    back = lax.all_to_all(sent_pages, ("z", "yl"), split_axis=0, concat_axis=0, tiled=True)
    fresh = pack_fresh(span_latent, span_rope, pair_latent, pair_rope)
    sent = split_queries(queries[0])
    lens = jnp.stack(
        [
            lax.dynamic_index_in_dim(cache_len, group, 0, keepdims=False),
            lax.dynamic_index_in_dim(span_len, group, 0, keepdims=False),
        ]
    )
    back, columns, fresh = lax.optimization_barrier((back, columns, fresh))
    weight = lax.all_gather(columns, "z", axis=0, tiled=False)
    mine = jnp.concatenate([back, swap_yh(back), fresh], 0)
    half = PIECE // 2
    left = step("x", 4, 1)(mine)
    right = step("x", 4, -1)(mine)
    exchanged = lax.all_to_all(sent, ("x", "yh", "c"), split_axis=0, concat_axis=0, tiled=True)
    mine_c = swap_c(mine)
    far_a = step("x", 4, 1)(left[:half])
    far_b = step("x", 4, -1)(right[half:])
    left_c, right_c = swap_c(left), swap_c(right)
    pieces = [mine, left, right, far_a, far_b, mine_c, left_c, right_c, swap_c(far_a), swap_c(far_b)]

    my_table = lax.dynamic_index_in_dim(page_table, group, 0, keepdims=False)
    source = my_table // slots
    before = (source[None, :] == source[:, None]) & (order[None, :] < order[:, None])
    place = jnp.minimum(jnp.sum(before.astype(jnp.int32), axis=1), 1)
    from_group = source // 16
    from_member = source % 16

    def piece_index(of_member):
        apart = (of_member // 4 - xi) % 4
        number = jnp.where(apart == 0, 0, jnp.where(apart == 3, 1, jnp.where(apart == 1, 2, 3)))
        return (jnp.where(of_member % 2 == ci, 0, 4) + number) * PIECE

    block = piece_index(from_member) + from_group + jnp.where((from_member // 2) % 2 == yh, 0, 16)
    members = jnp.arange(32, dtype=jnp.int32) // 2
    block_new = piece_index(members) + 32 + jnp.where((members // 2) % 2 == yh, 0, 1)
    index = jnp.concatenate([block * 2 + place, block_new * 2 + jnp.arange(32, dtype=jnp.int32) % 2])

    keys = assemble(index, pieces)
    exchanged, keys = lax.optimization_barrier((exchanged, keys))
    q = exchanged.reshape(SPAN, HEADS_HERE * QHEAD)
    own = [attend(half, lens, q, kv_up, keys) for half in range(2)]
    near = [swap_yl(x) for x in own]
    partial = project([*own, *near, *[swap_c(x) for x in own], *[swap_c(x) for x in near]], weight)
    shared = lax.all_to_all(partial, ("x", "yh"), split_axis=0, concat_axis=0, tiled=True)
    where = jnp.stack([yl, ci]).astype(jnp.int32)
    summed = jnp.sum(shared.astype(F32), axis=0).astype(BF).reshape(2, 2, OWN, 1792)
    own_rows = lax.dynamic_index_in_dim(summed, ci, 1, keepdims=False)
    mate_rows = lax.dynamic_index_in_dim(summed, 1 - ci, 1, keepdims=False)
    here, to_c, to_yl, to_both = own_rows[0], mate_rows[0], own_rows[1], mate_rows[1]
    from_both = lax.ppermute(to_both, ("yl", "c"), [(i, 3 - i) for i in range(4)])
    out = arrange(where, here, swap_c(to_c), swap_yl(to_yl), from_both)
    return out[None]


def solution(mesh):
    fine = Mesh(mesh.devices.reshape(8, 2, 4, 2, 2), ("z", "yl", "x", "yh", "c"))
    grp, head = ("z", "yl"), ("x", "yh", "c")
    return jax.shard_map(
        shards,
        mesh=fine,
        in_specs=(
            P(grp, head, None),
            P(grp, head, None),
            P(grp, head, None),
            P(grp + head, None, None),
            P(grp + head, None),
            P(),
            P(),
            P(),
            P(None, head),
            P(head, grp),
        ),
        out_specs=P(grp, head, None),
        check_vma=False,
    )
```
